512 devices in a mesh: ja: 16 (over y_hi, x, core), ia: 32 (over z, y_lo).
Axes of the slice: x: 4, y: 4 (y_hi: 2, y_lo: 2; y = y_hi * 2 + y_lo), z: 16, core: 2. Of those that a mesh axis runs over, the one named last changes fastest.
Arguments:
- potential_warmth: float32 [16, 1024, 4096], P(None, 'ja', 'ia'), may hold values from -2 to 30
- saltiness_psu: float32 [16, 1024, 4096], P(None, 'ja', 'ia'), may hold values from 33 to 37
- zonal_stability_ratio: float32 [16, 1024, 4096], P(None, 'ja', 'ia'), may hold values from -0.3 to 0.3
- poleward_stability_ratio: float32 [16, 1024, 4096], P(None, 'ja', 'ia'), may hold values from -0.3 to 0.3
- sinking_stability_ratio: float32 [16, 1024, 4096], P(None, 'ja', 'ia'), may hold values from -0.2 to 0.2
- seafloor_layer_index: int32 [1024, 4096], P('ja', 'ia'), may hold values from 0 to 16, as said below
Outputs:
- temperature_next: float32 [16, 1024, 4096], P(None, 'ja', 'ia')
- salinity_next: float32 [16, 1024, 4096], P(None, 'ja', 'ia')
The draws below stay inside these ranges and needn't reach their ends.
Inputs may be any that keep to these rules, and one draw needn't show every extreme that they name: Dry columns hold 0; a column is wet from the surface down to level seafloor_layer_index - 1; dry columns come in blocks of 32 rows by 64 columns.
All inputs are finite; a program needn't handle non-finite values.
Results may differ from the reference program's by a relative error of at most 0.0003.
Values sent between devices are 32-bit elements; how exact they have to be, the bound alone decides.
No kernel may reach another device: no remote copies, remote signals or barrier semaphores. Data moves between devices by JAX's collectives and lax.ppermute only.
A program may use at most 128 MiB of HBM per device.

```python
import jax
import jax.numpy as jnp
from jax import lax

DEPTH_LAYERS = 16
TILE_J = 64
TILE_I = 128
MESH_HEIGHT = 1024
MESH_WIDTH = 4096
N_JA = 16


def draw_seafloor_layer_index(key, part):
    key = jax.random.fold_in(key, 11)
    land_key, depth_key, jitter_key = jax.random.split(key, 3)
    land_rows = TILE_J // 2
    land_cols = TILE_I // 2
    depth_rows = TILE_J // 4
    depth_cols = TILE_I // 4
    coarse_land = jax.random.randint(land_key, (MESH_HEIGHT // land_rows, MESH_WIDTH // land_cols), 0, 3)
    coarse_land = jnp.repeat(jnp.repeat(coarse_land, land_rows, axis=0), land_cols, axis=1)
    coarse_depth = jax.random.randint(depth_key, (MESH_HEIGHT // depth_rows, MESH_WIDTH // depth_cols), 1, DEPTH_LAYERS + 2)
    coarse_depth = jnp.repeat(jnp.repeat(coarse_depth, depth_rows, axis=0), depth_cols, axis=1)
    jitter = jax.random.randint(jitter_key, (MESH_HEIGHT, MESH_WIDTH), -2, 3)
    depth = jnp.clip(coarse_depth + jitter, 1, DEPTH_LAYERS)
    return jnp.where(coarse_land == 0, 0, depth).astype(jnp.int32)


def level_of(stream_key, dims, cuts, smallest, largest):
    def one(axis_at, blocks):
        heights = jax.random.uniform(jax.random.fold_in(jax.random.fold_in(stream_key, 6), axis_at), (blocks,), jnp.float32, smallest / len(cuts), largest / len(cuts))
        return jnp.repeat(jnp.exp(heights), dims[axis_at] // blocks).reshape((-1,) + (1,) * (len(dims) - axis_at - 1))

    gain = one(*cuts[0])
    for cut in cuts[1:]:
        gain = gain * one(*cut)
    return gain


def setup_inputs(seed: int = 0) -> dict:
    keys = jax.random.split(jax.random.key(seed), 7)
    return {
        "potential_warmth": jnp.clip(-2.0 + 32.0 * jax.random.uniform(keys[0], (DEPTH_LAYERS, MESH_HEIGHT, MESH_WIDTH), jnp.float32) ** level_of(keys[0], (DEPTH_LAYERS, MESH_HEIGHT, MESH_WIDTH), ((1, 16), (2, 32)), -0.2, 0.2), -2.0, 30.0),
        "saltiness_psu": jnp.clip(33.0 + 4.0 * jax.random.uniform(keys[1], (DEPTH_LAYERS, MESH_HEIGHT, MESH_WIDTH), jnp.float32) ** level_of(keys[1], (DEPTH_LAYERS, MESH_HEIGHT, MESH_WIDTH), ((1, 16), (2, 32)), -0.2, 0.2), 33.0, 37.0),
        "zonal_stability_ratio": jnp.clip(jax.random.uniform(keys[2], (DEPTH_LAYERS, MESH_HEIGHT, MESH_WIDTH), jnp.float32, -0.3, 0.3) * level_of(keys[2], (DEPTH_LAYERS, MESH_HEIGHT, MESH_WIDTH), ((1, 16), (2, 32)), -0.4, 0.0), -0.3, 0.3),
        "poleward_stability_ratio": jnp.clip(jax.random.uniform(keys[3], (DEPTH_LAYERS, MESH_HEIGHT, MESH_WIDTH), jnp.float32, -0.3, 0.3) * level_of(keys[3], (DEPTH_LAYERS, MESH_HEIGHT, MESH_WIDTH), ((1, 16), (2, 32)), -0.4, 0.0), -0.3, 0.3),
        "sinking_stability_ratio": jnp.clip(jax.random.uniform(keys[4], (DEPTH_LAYERS, MESH_HEIGHT, MESH_WIDTH), jnp.float32, -0.2, 0.2) * level_of(keys[4], (DEPTH_LAYERS, MESH_HEIGHT, MESH_WIDTH), ((1, 16), (2, 32)), -0.4, 0.0), -0.2, 0.2),
        "seafloor_layer_index": draw_seafloor_layer_index(jax.random.fold_in(keys[6], 71), 0),
    }


THERMAL_COEF = 0.1655
HALINE_COEF = 0.76554
CABBELING_T = 0.05952
CABBELING_S = 0.00054914
THERMOBARIC_T = 0.0001497
THERMOBARIC_S = 0.00001109
MIXED_COEF = 0.0024341
LAYER_DEPTH = 50.0
MIXING_BASE = 0.5
MIXING_CONV = 10.0
DENSITY_SCALE = 0.5


def take_slab(array, offset, length, along):
    return lax.slice_in_dim(array, offset, offset + length, axis=along % array.ndim)


def min_modulus(left_slope, right_slope):
    return 0.5 * (jnp.sign(left_slope) + jnp.sign(right_slope)) * jnp.minimum(jnp.abs(left_slope), jnp.abs(right_slope))


def tvd_divergence(scalar_quantity, seawater_indicator, stability_ratio, along):
    count = scalar_quantity.shape[along % scalar_quantity.ndim] - 4
    face_wet = take_slab(seawater_indicator, 0, count + 3, along) * take_slab(seawater_indicator, 1, count + 3, along)
    slopes = face_wet * (take_slab(scalar_quantity, 1, count + 3, along) - take_slab(scalar_quantity, 0, count + 3, along))
    centre = take_slab(slopes, 1, count + 1, along)
    below_face = take_slab(slopes, 0, count + 1, along)
    above_face = take_slab(slopes, 2, count + 1, along)
    open_face = take_slab(face_wet, 1, count + 1, along)
    upwind_left = take_slab(scalar_quantity, 1, count + 1, along)
    upwind_right = take_slab(scalar_quantity, 2, count + 1, along)
    damping = 0.5 * (1.0 - jnp.abs(stability_ratio))
    face_value = jnp.where(stability_ratio > 0, upwind_left + damping * min_modulus(centre, below_face),
                          upwind_right - damping * min_modulus(centre, above_face))
    flux = stability_ratio * open_face * face_value
    return take_slab(flux, 1, count, along) - take_slab(flux, 0, count, along)


def density(temp_star, salt_star, depth):
    anomaly_t = temp_star - 10.0
    anomaly_s = salt_star - 35.0
    return (-THERMAL_COEF * (1.0 + 0.5 * CABBELING_T * anomaly_t + THERMOBARIC_T * depth) * anomaly_t
            + HALINE_COEF * (1.0 - 0.5 * CABBELING_S * anomaly_s - THERMOBARIC_S * depth) * anomaly_s
            - MIXED_COEF * anomaly_t * anomaly_s)


def column_mixing_physics(scalar_quantities, horizontal_part, down_faces, seawater_indicator):
    layer_total = scalar_quantities.shape[1]
    depth = (LAYER_DEPTH * (jnp.arange(layer_total, dtype=jnp.float32) + 0.5))[:, None, None]
    padded = jnp.pad(scalar_quantities, ((0, 0), (2, 2), (0, 0), (0, 0)))
    wet_padded = jnp.pad(seawater_indicator, ((2, 2), (0, 0), (0, 0)))
    faces = jnp.pad(down_faces[:-1], ((1, 1), (0, 0), (0, 0)))
    vertical = tvd_divergence(padded, wet_padded, faces, -3)
    star = seawater_indicator * (scalar_quantities - horizontal_part - vertical)
    density_now = density(star[0], star[1], depth)
    density_jump = density_now[1:] - density_now[:-1]
    mixing = seawater_indicator[:-1] * seawater_indicator[1:] * (MIXING_BASE + MIXING_CONV * jax.nn.sigmoid(-density_jump / DENSITY_SCALE))
    ratio_prev = jnp.zeros(star.shape[2:], jnp.float32)
    value_prev = jnp.zeros(star[:, 0].shape, jnp.float32)
    ratios = []
    values = []
    for layer_index in range(layer_total):
        above = mixing[layer_index - 1] if layer_index > 0 else jnp.zeros(star.shape[2:], jnp.float32)
        below = mixing[layer_index] if layer_index < layer_total - 1 else jnp.zeros(star.shape[2:], jnp.float32)
        pivot_value = 1.0 + above + below - above * ratio_prev
        value_prev = (star[:, layer_index] + above * value_prev) / pivot_value
        ratio_prev = below / pivot_value
        ratios.append(ratio_prev)
        values.append(value_prev)
    solved = [None] * layer_total
    solved[layer_total - 1] = values[layer_total - 1]
    for layer_index in range(layer_total - 2, -1, -1):
        solved[layer_index] = values[layer_index] + ratios[layer_index] * solved[layer_index + 1]
    return seawater_indicator * jnp.stack(solved, axis=1)


def reference(potential_warmth, saltiness_psu, zonal_stability_ratio, poleward_stability_ratio, sinking_stability_ratio, seafloor_layer_index):
    level_ids = jnp.arange(DEPTH_LAYERS, dtype=jnp.int32)[:, None, None]
    seawater_indicator = (level_ids < seafloor_layer_index[None]).astype(jnp.float32)

    def horizontal(layer_index):
        scalar_quantity = jnp.stack([potential_warmth[layer_index], saltiness_psu[layer_index]])
        wet_level = seawater_indicator[layer_index]
        east = zonal_stability_ratio[layer_index]
        north = poleward_stability_ratio[layer_index]
        zonal_q = jnp.concatenate([scalar_quantity[:, :, -2:], scalar_quantity, scalar_quantity[:, :, :2]], axis=2)
        zonal_w = jnp.concatenate([wet_level[:, -2:], wet_level, wet_level[:, :2]], axis=1)
        zonal_c = jnp.concatenate([east[:, -1:], east], axis=1)
        fold_q = jnp.flip(scalar_quantity[:, MESH_HEIGHT - 2:, :], axis=(1, 2))
        fold_w = jnp.flip(wet_level[MESH_HEIGHT - 2:, :], axis=(0, 1))
        merid_q = jnp.concatenate([jnp.zeros((2, 2, MESH_WIDTH), jnp.float32), scalar_quantity, fold_q], axis=1)
        merid_w = jnp.concatenate([jnp.zeros((2, MESH_WIDTH), jnp.float32), wet_level, fold_w], axis=0)
        fold_face = 0.5 * (north[MESH_HEIGHT - 1] - north[MESH_HEIGHT - 1, ::-1])
        merid_c = jnp.concatenate([jnp.zeros((1, MESH_WIDTH), jnp.float32), north[:MESH_HEIGHT - 1], fold_face[None]], axis=0)
        return tvd_divergence(zonal_q, zonal_w, zonal_c, -1) + tvd_divergence(merid_q, merid_w, merid_c, -2)

    horizontal_part = lax.map(horizontal, jnp.arange(DEPTH_LAYERS, dtype=jnp.int32))
    horizontal_part = jnp.transpose(horizontal_part, (1, 0, 2, 3))
    scalar_quantities = jnp.stack([potential_warmth, saltiness_psu])

    def block_rows(block):
        offset = (block * TILE_J).astype(jnp.int32)
        return column_mixing_physics(lax.dynamic_slice_in_dim(scalar_quantities, offset, TILE_J, 2),
                              lax.dynamic_slice_in_dim(horizontal_part, offset, TILE_J, 2),
                              lax.dynamic_slice_in_dim(sinking_stability_ratio, offset, TILE_J, 1),
                              lax.dynamic_slice_in_dim(seawater_indicator, offset, TILE_J, 1))

    blocks = lax.map(block_rows, jnp.arange(N_JA, dtype=jnp.int32))
    step_output = jnp.transpose(blocks, (1, 2, 0, 3, 4)).reshape(2, DEPTH_LAYERS, MESH_HEIGHT, MESH_WIDTH)
    return step_output[0], step_output[1]
```

```python
import functools

import jax
import jax.numpy as jnp
from jax import lax
from jax.experimental import pallas as pl
from jax.experimental.pallas import tpu as pltpu
from jax.sharding import PartitionSpec as P

THERMAL_COEF = 0.1655
HALINE_COEF = 0.76554
CABBELING_T = 0.05952
CABBELING_S = 0.00054914
THERMOBARIC_T = 0.0001497
THERMOBARIC_S = 1.109e-05
MIXED_COEF = 0.0024341
LAYER_DEPTH = 50.0

NK = 16
NJ = 64
NI = 128
NB = NJ // 8
F32 = jnp.float32

COLS = (-3, -2, -1, 0, 1, 2)
ROWS = (0, 1, 2, 61, 62, 63)
MROWS = 88


def lanes():
    return lax.broadcasted_iota(jnp.int32, (8, NI), 1)


def sublanes():
    return lax.broadcasted_iota(jnp.int32, (8, NI), 0)


def minmod(x, y):
    return jnp.maximum(jnp.minimum(x, jnp.maximum(y, 0.0)), jnp.minimum(y, 0.0))


def slope_factor(c):
    return jnp.where(c > 0, 0.5, -0.5) - 0.5 * c


def flux(c, c_open, factor, qa, sa, qb, sb):
    up = c > 0
    return c_open * (jnp.where(up, qa, qb) + factor * jnp.where(up, sa, sb))


def pack_kernel(
    t_hbm, s_hbm, u_hbm, v_hbm, w_hbm, k_hbm, east_ref, west_ref, p1_ref, p2_ref, own_ref,
    t_ref, s_ref, u_ref, v_ref, w_ref, k_ref, sems,
):
    chunks = 4
    per = NK // chunks
    copies = []
    for c in range(chunks):
        part = pl.ds(c * per, per)
        for f, (src, dst) in enumerate(((t_hbm, t_ref), (s_hbm, s_ref), (u_hbm, u_ref))):
            copies.append(pltpu.make_async_copy(src.at[part], dst.at[part], sems.at[c * 3 + f]))
    late = [
        pltpu.make_async_copy(k_hbm, k_ref, sems.at[12]),
        pltpu.make_async_copy(v_hbm, v_ref, sems.at[13]),
        pltpu.make_async_copy(w_hbm, w_ref, sems.at[14]),
    ]
    for c in copies + late:
        c.start()

    lane = lanes()
    even = lax.rem(lax.axis_index("ja"), 2) == 0
    near1 = jnp.where(even, NJ - 1, 0)
    far1 = jnp.where(even, NJ - 2, 1)
    near2 = jnp.where(even, 0, NJ - 1)
    far2 = jnp.where(even, 1, NJ - 2)
    rows = ((p1_ref, near1, far1), (p2_ref, near2, far2))

    def windows(blocks, k, window):
        out = pltpu.roll(blocks[0], k, 1)
        for b in range(1, NB):
            out = jnp.where(window == b, pltpu.roll(blocks[b], b * 16 + k, 1), out)
        return out

    t_acc = [None] * 6
    s_acc = [None] * 6
    u_acc = [None] * 6
    for k in range(NK):
        if k % per == 0:
            for c in copies[k // per * 3 : k // per * 3 + 3]:
                c.wait()
        place = (lane - (k - 3)) & (NI - 1)
        window = lax.shift_right_logical(place, 4)
        within = place & 15
        for ref, acc, which in ((t_ref, t_acc, range(6)), (s_ref, s_acc, range(6)), (u_ref, u_acc, (1, 2, 3))):
            got = windows([ref[k, pl.ds(8 * b, 8), :] for b in range(NB)], k, window)
            for n in which:
                acc[n] = got if k == 0 else jnp.where(within == n, got, acc[n])
        for ref, near, far in rows:
            ref[pl.ds(k, 1), :] = t_ref[k, pl.ds(near, 1), :]
            ref[pl.ds(16 + k, 1), :] = t_ref[k, pl.ds(far, 1), :]
            ref[pl.ds(32 + k, 1), :] = s_ref[k, pl.ds(near, 1), :]
            ref[pl.ds(48 + k, 1), :] = s_ref[k, pl.ds(far, 1), :]
    for c in late:
        c.wait()
    for ref, near, far in rows:
        for k in range(NK):
            ref[pl.ds(64 + k, 1), :] = v_ref[k, pl.ds(near, 1), :]
        ref[pl.ds(80, 8), :] = jnp.zeros((8, NI), F32)
        ref[pl.ds(80, 1), :] = k_ref[pl.ds(near, 1), :].astype(F32)
        ref[pl.ds(81, 1), :] = k_ref[pl.ds(far, 1), :].astype(F32)

    place = (lane + 3) & (NI - 1)
    floor = windows([k_ref[pl.ds(8 * b, 8), :].astype(F32) for b in range(NB)], 0, lax.shift_right_logical(place, 4))
    first = (lane & 15) == 0
    k_cols = []
    for n, off in enumerate(COLS):
        x = jnp.where(first, pltpu.roll(floor, -off % NI, 1), 0.0)
        for step in (1, 2, 4, 8):
            x = x + pltpu.roll(x, step, 1)
        k_cols.append(x)
    t_cols = [pltpu.roll(x, -off % NI, 1) for x, off in zip(t_acc, COLS)]
    s_cols = [pltpu.roll(x, -off % NI, 1) for x, off in zip(s_acc, COLS)]
    u_cols = [pltpu.roll(u_acc[n], -COLS[n] % NI, 1) for n in (1, 2, 3)]
    for n, x in enumerate(t_cols + s_cols + k_cols + u_cols):
        own_ref[n] = x
    for n, x in enumerate((t_cols[2], t_cols[1], s_cols[2], s_cols[1], k_cols[2], k_cols[1], u_cols[1])):
        east_ref[n] = x
    for n, x in enumerate((t_cols[3], t_cols[4], s_cols[3], s_cols[4], k_cols[3], k_cols[4])):
        west_ref[n] = x


def pack(t, s, u, v, w, floor):
    fields = [pltpu.with_memory_space_constraint(x, pltpu.HBM) for x in (t, s, u, v, w, floor)]
    return pl.pallas_call(
        pack_kernel,
        out_shape=tuple(
            pltpu.VMEM(shape, F32) for shape in ((7, 8, NI), (6, 8, NI), (MROWS, NI), (MROWS, NI), (21, 8, NI))
        )
        + (pltpu.VMEM((NK, NJ, NI), F32),) * 5
        + (pltpu.VMEM((NJ, NI), jnp.int32),),
        in_specs=[pl.BlockSpec(memory_space=pltpu.HBM)] * 6,
        out_specs=(pl.BlockSpec(memory_space=pltpu.VMEM),) * 11,
        scratch_shapes=[pltpu.SemaphoreType.DMA((15,))],
        compiler_params=pltpu.CompilerParams(vmem_limit_bytes=16 * 2**20),
        name="pack_edges",
    )(*fields)


def bulk_kernel(t_ref, s_ref, u_ref, v_ref, w_ref, k_ref, to_ref, so_ref, rows_ref, th_ref, sh_ref, mask_ref):
    lane = lanes()
    sub = sublanes()
    floors = [k_ref[pl.ds(m, 8, stride=8), :] for m in range(NB)]
    for m in range(NB):
        east = jnp.where(lane == NI - 1, 0, jnp.minimum(floors[m], pltpu.roll(floors[m], NI - 1, 1)))
        if m < NB - 1:
            north = jnp.minimum(floors[m], floors[m + 1])
        else:
            north = jnp.where(sub == 7, 0, jnp.minimum(floors[m], pltpu.roll(floors[0], 7, 0)))
        mask_ref[0, m] = east
        mask_ref[1, m] = jnp.where((lane == 0) | (lane == NI - 2), 0, east)
        mask_ref[2, m] = north
        inner = north
        if m == 0:
            inner = jnp.where(sub == 0, 0, inner)
        if m == NB - 2:
            inner = jnp.where(sub == 7, 0, inner)
        mask_ref[3, m] = inner

    def level(k):
        q = [[ref[k, pl.ds(m, 8, stride=8), :] for m in range(NB)] for ref in (t_ref, s_ref)]
        c = [v_ref[k, pl.ds(m, 8, stride=8), :] for m in range(NB)]
        c_open = [jnp.where(mask_ref[3, m] > k, c[m], 0.0) for m in range(NB)]
        is_open = [mask_ref[2, m] > k for m in range(NB)]
        factor = [slope_factor(x) for x in c]
        left = []
        for x in q:
            after = x[1:] + [pltpu.roll(x[0], 7, 0)]
            g = [jnp.where(o, b - a, 0.0) for o, a, b in zip(is_open, x, after)]
            g_before = [pltpu.roll(g[-1], 1, 0)] + g[:-1]
            slope = [minmod(a, b) for a, b in zip(g, g_before)]
            slope_after = slope[1:] + [pltpu.roll(slope[0], 7, 0)]
            f = [flux(*y) for y in zip(c, c_open, factor, x, slope, after, slope_after)]
            f_before = [pltpu.roll(f[-1], 1, 0)] + f[:-1]
            left.append([a - (b - d) for a, b, d in zip(x, f, f_before)])
        for m in range(NB):
            c = u_ref[k, pl.ds(m, 8, stride=8), :]
            c_open = jnp.where(mask_ref[1, m] > k, c, 0.0)
            is_open = mask_ref[0, m] > k
            factor = slope_factor(c)
            for n, out in ((0, th_ref), (1, sh_ref)):
                x = q[n][m]
                after = pltpu.roll(x, NI - 1, 1)
                g = jnp.where(is_open, after - x, 0.0)
                slope = minmod(g, pltpu.roll(g, 1, 1))
                f = flux(c, c_open, factor, x, slope, after, pltpu.roll(slope, NI - 1, 1))
                out[k, pl.ds(m, 8, stride=8), :] = left[n][m] - (f - pltpu.roll(f, 1, 1))

    @pl.loop(0, NK, unroll=4)
    def _(k):
        level(k)

    def column(b, _):
        at = pl.ds(pl.multiple_of(b * 8, 8), 8)
        floor = k_ref[at, :]
        c = [w_ref[k, at, :] for k in range(NK - 1)]
        is_open = [floor > k + 1 for k in range(NK - 1)]
        c_open = [jnp.where(o, x, 0.0) for o, x in zip(is_open, c)]
        factor = [slope_factor(x) for x in c]
        for src, half, out in ((t_ref, th_ref, to_ref), (s_ref, sh_ref, so_ref)):
            x = [src[k, at, :] for k in range(NK)]
            g = [jnp.where(is_open[k], x[k + 1] - x[k], 0.0) for k in range(NK - 1)]
            slope = [jnp.zeros((8, NI), F32)] + [minmod(g[k], g[k - 1]) for k in range(1, NK - 1)] + [jnp.zeros((8, NI), F32)]
            before = None
            for k in range(NK):
                y = half[k, at, :]
                if k < NK - 1:
                    f = flux(c[k], c_open[k], factor[k], x[k], slope[k], x[k + 1], slope[k + 1])
                    y = y - (f if before is None else f - before)
                    before = f
                else:
                    y = y + before
                out[k, at, :] = y
        return 0

    lax.fori_loop(0, NB, column, 0)

    for n, r in enumerate(ROWS):
        for k in range(NK):
            rows_ref[n, pl.ds(k, 1), :] = t_ref[k, pl.ds(r, 1), :]
            rows_ref[6 + n, pl.ds(k, 1), :] = s_ref[k, pl.ds(r, 1), :]
    for n, r in enumerate((0, 62, 63)):
        for k in range(NK):
            rows_ref[12 + n, pl.ds(k, 1), :] = v_ref[k, pl.ds(r, 1), :]


def bulk(t, s, u, v, w, floor):
    vmem = pl.BlockSpec(memory_space=pltpu.VMEM)
    field = pltpu.VMEM((NK, NJ, NI), F32)
    return pl.pallas_call(
        bulk_kernel,
        out_shape=(
            pltpu.VMEM((NK, NJ, NI), F32),
            pltpu.VMEM((NK, NJ, NI), F32),
            pltpu.VMEM((15, NK, NI), F32),
        ),
        in_specs=[vmem] * 6,
        out_specs=(vmem,) * 3,
        scratch_shapes=[field, field, pltpu.VMEM((4, NB, 8, NI), jnp.int32)],
        compiler_params=pltpu.CompilerParams(vmem_limit_bytes=16 * 2**20),
        cost_estimate=pl.CostEstimate(flops=16_000_000, bytes_accessed=4_000_000, transcendentals=0),
        name="bulk_fluxes",
    )(t, s, u, v, w, floor)


def edge_fluxes(level, q, floor, c):
    is_open = [level < jnp.minimum(a, b) for a, b in zip(floor, floor[1:])]
    g = [jnp.where(o, b - a, 0.0) for o, a, b in zip(is_open, q, q[1:])]
    slope = [None] + [minmod(a, b) for a, b in zip(g, g[1:])]
    out = []
    for n, x in zip((1, 2), c):
        out.append(flux(x, jnp.where(is_open[n], x, 0.0), slope_factor(x), q[n], slope[n], q[n + 1], slope[n + 1]))
    return out


def solve_kernel(
    ts_ref, ss_ref, k_ref, own_ref, east_ref, west_ref, p1_ref, p2_ref, rows_ref, tn_hbm, sn_hbm,
    to_ref, so_ref, zonal_ref, merid_ref, out_sems,
):
    lane = lanes()
    ja = lax.axis_index("ja")
    even = lax.rem(ja, 2) == 0
    is_north = ja == lax.axis_size("ja") - 1

    level = (lane & 15).astype(F32)
    own = [own_ref[n] for n in range(21)]
    k_own = own[12:18]
    u_own = own[18:21]
    west_floor = [east_ref[5], east_ref[4]] + k_own[3:6]
    east_floor = k_own[0:3] + [west_ref[4], west_ref[5]]
    for n in range(2):
        q = own[6 * n : 6 * n + 6]
        f0, f1 = edge_fluxes(level, [east_ref[2 * n + 1], east_ref[2 * n]] + q[3:6], west_floor, (east_ref[6], u_own[2]))
        f2, f3 = edge_fluxes(level, q[0:3] + [west_ref[2 * n], west_ref[2 * n + 1]], east_floor, (u_own[0], u_own[1]))
        parts = (f2, f3 - f2, f1 - f0, -f1)
        for r in range(4):
            x = parts[0] if r == 0 else pltpu.roll(parts[0], (0 - r) % NI, 1)
            for i in range(1, 4):
                moved = parts[i] if i == r else pltpu.roll(parts[i], (i - r) % NI, 1)
                x = jnp.where((lane & 3) == i, moved, x)
            zonal_ref[n, r] = x

    level = lax.broadcasted_iota(jnp.int32, (NK, NI), 0).astype(F32)
    turned = NI - 1 - lanes()
    p1 = [p1_ref[pl.ds(8 * n, 8), :] for n in range(MROWS // 8)]
    p2 = [p2_ref[pl.ds(8 * n, 8), :] for n in range(MROWS // 8)]
    south = [jnp.where(even, b, a) for a, b in zip(p1, p2)]
    north = [jnp.where(is_north, jnp.take_along_axis(b, turned, axis=1), jnp.where(even, a, b)) for a, b in zip(p1, p2)]

    def plane(msg, n):
        return jnp.concatenate([msg[2 * n], msg[2 * n + 1]], axis=0)

    def wide(row):
        return jnp.broadcast_to(row, (NK, NI))

    floors = [wide(k_ref[pl.ds(r, 1), :].astype(F32)) for r in ROWS]
    s_floor = [wide(south[10][1:2]), wide(south[10][0:1])] + floors[0:3]
    n_floor = floors[3:6] + [wide(north[10][0:1]), wide(north[10][1:2])]
    last = jnp.where(is_north, 0.5 * (rows_ref[14] - plane(north, 4)), rows_ref[14])
    merid_ref[...] = jnp.zeros_like(merid_ref)
    for n in range(2):
        q = [rows_ref[6 * n + r] for r in range(6)]
        f0, f1 = edge_fluxes(level, [plane(south, 2 * n + 1), plane(south, 2 * n)] + q[0:3], s_floor, (plane(south, 4), rows_ref[12]))
        f2, f3 = edge_fluxes(level, q[3:6] + [plane(north, 2 * n), plane(north, 2 * n + 1)], n_floor, (rows_ref[13], last))
        for side, r, x in ((0, 0, f1 - f0), (0, 1, -f1), (2, 6, f2), (2, 7, f3 - f2)):
            for k in range(NK):
                merid_ref[n, side, k, pl.ds(r, 1), :] = x[k : k + 1]

    edge_lanes = (lane < 2) | (lane >= NI - 2)

    def column(b, _):
        at = pl.ds(pl.multiple_of(b * 8, 8), 8)
        side = jnp.where(b == 0, 0, jnp.where(b == NB - 1, 2, 1))
        floor = k_ref[at, :]
        wet = [floor > k for k in range(NK)]
        star = []
        for n, ref in enumerate((ts_ref, ss_ref)):
            star.append([])
            for k in range(NK):
                amount = lax.rem(2 * NI - 2 - 4 * (k // 4) - 16 * b, NI)
                z = pltpu.roll(zonal_ref[n, k % 4], amount, 1)
                x = ref[k, at, :] - (jnp.where(edge_lanes, z, 0.0) + merid_ref[n, side, k])
                star[n].append(jnp.where(wet[k], x, 0.0))
        dens = []
        for k in range(NK):
            z = LAYER_DEPTH * (k + 0.5)
            ta = star[0][k] - 10.0
            sa = star[1][k] - 35.0
            heat = (-0.5 * THERMAL_COEF * CABBELING_T) * ta - MIXED_COEF * sa - THERMAL_COEF * (1.0 + THERMOBARIC_T * z)
            salt = (-0.5 * HALINE_COEF * CABBELING_S) * sa + HALINE_COEF * (1.0 - THERMOBARIC_S * z)
            dens.append(heat * ta + salt * sa)
        above = None
        ratio = []
        values = ([], [])
        for k in range(NK):
            if k < NK - 1:
                below = jnp.where(wet[k + 1], 5.5 - 5.0 * jnp.tanh(dens[k + 1] - dens[k]), 0.0)
                pivot = 1.0 + below
            else:
                below = None
                pivot = 1.0
            if k > 0:
                pivot = pivot + above * (1.0 - ratio[-1])
            r = pl.reciprocal(pivot, approx=True)
            r = r * (2.0 - pivot * r)
            if below is not None:
                ratio.append(below * r)
            for n in range(2):
                x = star[n][k]
                if k > 0:
                    x = x + above * values[n][-1]
                values[n].append(x * r)
            above = below
        for n, out in enumerate((to_ref, so_ref)):
            x = values[n][NK - 1]
            out[NK - 1, at, :] = jnp.where(wet[NK - 1], x, 0.0)
            for k in range(NK - 2, -1, -1):
                x = values[n][k] + ratio[k] * x
                out[k, at, :] = jnp.where(wet[k], x, 0.0)
        pltpu.make_async_copy(to_ref.at[:, at], tn_hbm.at[:, at], out_sems.at[0, b]).start()
        pltpu.make_async_copy(so_ref.at[:, at], sn_hbm.at[:, at], out_sems.at[1, b]).start()
        return 0

    lax.fori_loop(0, NB, column, 0)
    for b in range(NB):
        at = pl.ds(b * 8, 8)
        pltpu.make_async_copy(to_ref.at[:, at], tn_hbm.at[:, at], out_sems.at[0, b]).wait()
        pltpu.make_async_copy(so_ref.at[:, at], sn_hbm.at[:, at], out_sems.at[1, b]).wait()


def solve(ts, ss, floor, own, east, west, p1, p2, rows):
    any_ = pl.BlockSpec(memory_space=pltpu.HBM)
    vmem = pl.BlockSpec(memory_space=pltpu.VMEM)
    field = pltpu.VMEM((NK, NJ, NI), F32)
    return pl.pallas_call(
        solve_kernel,
        out_shape=(jax.ShapeDtypeStruct((NK, NJ, NI), F32),) * 2,
        in_specs=[vmem] * 9,
        out_specs=(any_, any_),
        scratch_shapes=[field] * 2
        + [
            pltpu.VMEM((2, 4, 8, NI), F32),
            pltpu.VMEM((2, 3, NK, 8, NI), F32),
            pltpu.SemaphoreType.DMA((2, NB)),
        ],
        compiler_params=pltpu.CompilerParams(vmem_limit_bytes=16 * 2**20),
        cost_estimate=pl.CostEstimate(flops=6_000_000, bytes_accessed=2_500_000, transcendentals=300_000),
        name="solve_columns",
    )(ts, ss, floor, own, east, west, p1, p2, rows)


def local(nj, ni, t, s, u, v, w, floor):
    east, west, p1, p2, own, t, s, u, v, w, floor = pack(t, s, u, v, w, floor)
    east_pairs = [(i, (i + 1) % ni) for i in range(ni)]
    west_pairs = [((i + 1) % ni, i) for i in range(ni)]
    first = []
    second = []
    for i in range(ni):
        for j in range(0, nj, 2):
            first += [(j * ni + i, (j + 1) * ni + i), ((j + 1) * ni + i, j * ni + i)]
        for j in range(1, nj - 1, 2):
            second += [(j * ni + i, (j + 1) * ni + i), ((j + 1) * ni + i, j * ni + i)]
        second.append(((nj - 1) * ni + i, (nj - 1) * ni + ni - 1 - i))
    from_west = lax.ppermute(east, "ia", east_pairs)
    q1 = lax.ppermute(p1, ("ja", "ia"), first)
    q2 = lax.ppermute(p2, ("ja", "ia"), second)
    from_east = lax.ppermute(west, "ia", west_pairs)
    ts, ss, rows = bulk(t, s, u, v, w, floor)
    return solve(ts, ss, floor, own, from_west, from_east, q1, q2, rows)


def solution(mesh):
    field = P(None, "ja", "ia")
    return jax.shard_map(
        functools.partial(local, mesh.shape["ja"], mesh.shape["ia"]),
        mesh=mesh,
        in_specs=(field,) * 5 + (P("ja", "ia"),),
        out_specs=(field, field),
        check_vma=False,
    )
```

```python
import functools

import jax
import jax.numpy as jnp
from jax import lax
from jax.experimental import pallas as pl
from jax.experimental.pallas import tpu as pltpu
from jax.sharding import PartitionSpec as P

THERMAL_COEF = 0.1655
HALINE_COEF = 0.76554
CABBELING_T = 0.05952
CABBELING_S = 0.00054914
THERMOBARIC_T = 0.0001497
THERMOBARIC_S = 1.109e-05
MIXED_COEF = 0.0024341
LAYER_DEPTH = 50.0

NK = 16
NJ = 64
NI = 128
NB = NJ // 8
SOLVE_ROWS = 32
F32 = jnp.float32

COLS = (-3, -2, -1, 0, 1, 2)
ROWS = (0, 1, 2, 61, 62, 63)
MROWS = 88


def lanes():
    return lax.broadcasted_iota(jnp.int32, (8, NI), 1)


def sublanes():
    return lax.broadcasted_iota(jnp.int32, (8, NI), 0)


def minmod(x, y):
    return jnp.maximum(jnp.minimum(x, jnp.maximum(y, 0.0)), jnp.minimum(y, 0.0))


def slope_factor(c):
    return jnp.where(c > 0, 0.5, -0.5) - 0.5 * c


def flux(c, c_open, factor, qa, sa, qb, sb):
    up = c > 0
    return c_open * (jnp.where(up, qa, qb) + factor * jnp.where(up, sa, sb))


def bulk_fluxes(t_ref, s_ref, u_ref, v_ref, w_hbm, k_ref, to_ref, so_ref, w_ref, th_ref, sh_ref, mask_ref, sem):
    w_copy = pltpu.make_async_copy(w_hbm, w_ref, sem)
    w_copy.start()
    lane = lanes()
    sub = sublanes()
    floors = [k_ref[pl.ds(m, 8, stride=8), :] for m in range(NB)]
    for m in range(NB):
        east = jnp.where(lane == NI - 1, 0, jnp.minimum(floors[m], pltpu.roll(floors[m], NI - 1, 1)))
        if m < NB - 1:
            north = jnp.minimum(floors[m], floors[m + 1])
        else:
            north = jnp.where(sub == 7, 0, jnp.minimum(floors[m], pltpu.roll(floors[0], 7, 0)))
        mask_ref[0, m] = east
        mask_ref[1, m] = jnp.where((lane == 0) | (lane == NI - 2), 0, east)
        mask_ref[2, m] = north
        inner = north
        if m == 0:
            inner = jnp.where(sub == 0, 0, inner)
        if m == NB - 2:
            inner = jnp.where(sub == 7, 0, inner)
        mask_ref[3, m] = inner

    def level(k):
        q = [[ref[k, pl.ds(m, 8, stride=8), :] for m in range(NB)] for ref in (t_ref, s_ref)]
        c = [v_ref[k, pl.ds(m, 8, stride=8), :] for m in range(NB)]
        c_open = [jnp.where(mask_ref[3, m] > k, c[m], 0.0) for m in range(NB)]
        is_open = [mask_ref[2, m] > k for m in range(NB)]
        factor = [slope_factor(x) for x in c]
        left = []
        for x in q:
            after = x[1:] + [pltpu.roll(x[0], 7, 0)]
            g = [jnp.where(o, b - a, 0.0) for o, a, b in zip(is_open, x, after)]
            g_before = [pltpu.roll(g[-1], 1, 0)] + g[:-1]
            slope = [minmod(a, b) for a, b in zip(g, g_before)]
            slope_after = slope[1:] + [pltpu.roll(slope[0], 7, 0)]
            f = [flux(*y) for y in zip(c, c_open, factor, x, slope, after, slope_after)]
            f_before = [pltpu.roll(f[-1], 1, 0)] + f[:-1]
            left.append([a - (b - d) for a, b, d in zip(x, f, f_before)])
        for m in range(NB):
            c = u_ref[k, pl.ds(m, 8, stride=8), :]
            c_open = jnp.where(mask_ref[1, m] > k, c, 0.0)
            is_open = mask_ref[0, m] > k
            factor = slope_factor(c)
            for n, out in ((0, th_ref), (1, sh_ref)):
                x = q[n][m]
                after = pltpu.roll(x, NI - 1, 1)
                g = jnp.where(is_open, after - x, 0.0)
                slope = minmod(g, pltpu.roll(g, 1, 1))
                f = flux(c, c_open, factor, x, slope, after, pltpu.roll(slope, NI - 1, 1))
                out[k, pl.ds(m, 8, stride=8), :] = left[n][m] - (f - pltpu.roll(f, 1, 1))

    @pl.loop(0, NK, unroll=4)
    def _(k):
        level(k)

    w_copy.wait()

    def column(b, _):
        at = pl.ds(pl.multiple_of(b * 8, 8), 8)
        floor = k_ref[at, :]
        c = [w_ref[k, at, :] for k in range(NK - 1)]
        is_open = [floor > k + 1 for k in range(NK - 1)]
        c_open = [jnp.where(o, x, 0.0) for o, x in zip(is_open, c)]
        factor = [slope_factor(x) for x in c]
        for src, half, out in ((t_ref, th_ref, to_ref), (s_ref, sh_ref, so_ref)):
            x = [src[k, at, :] for k in range(NK)]
            g = [jnp.where(is_open[k], x[k + 1] - x[k], 0.0) for k in range(NK - 1)]
            slope = [jnp.zeros((8, NI), F32)] + [minmod(g[k], g[k - 1]) for k in range(1, NK - 1)] + [jnp.zeros((8, NI), F32)]
            before = None
            for k in range(NK):
                y = half[k, at, :]
                if k < NK - 1:
                    f = flux(c[k], c_open[k], factor[k], x[k], slope[k], x[k + 1], slope[k + 1])
                    y = y - (f if before is None else f - before)
                    before = f
                else:
                    y = y + before
                out[k, at, :] = y
        return 0

    lax.fori_loop(0, NB, column, 0)


def bulk_scratch():
    field = pltpu.VMEM((NK, NJ, NI), F32)
    return [field, field, field, pltpu.VMEM((4, NB, 8, NI), jnp.int32), pltpu.SemaphoreType.DMA(())]


def bulk_first():
    ja, ia = lax.axis_index("ja"), lax.axis_index("ia")
    ni = lax.axis_size("ia")
    near_fold = ja >= lax.axis_size("ja") - 2
    return ia < jnp.where(near_fold, 3 * ni // 8, ni // 8)


def pack_kernel(
    t_hbm, s_hbm, u_hbm, v_hbm, w_hbm, k_hbm, p2_ref, east_ref, west_ref, p1_ref, own_ref,
    t_ref, s_ref, u_ref, v_ref, k_ref, ts_ref, ss_ref, sems, *scratch,
):
    chunks = 4
    per = NK // chunks
    copies = []
    for c in range(chunks):
        part = pl.ds(c * per, per)
        for f, (src, dst) in enumerate(((t_hbm, t_ref), (s_hbm, s_ref), (u_hbm, u_ref))):
            copies.append(pltpu.make_async_copy(src.at[part], dst.at[part], sems.at[c * 3 + f]))
    early = [
        pltpu.make_async_copy(k_hbm, k_ref, sems.at[12]),
        pltpu.make_async_copy(v_hbm, v_ref, sems.at[13]),
    ]
    for c in early + copies:
        c.start()

    lane = lanes()
    even = lax.rem(lax.axis_index("ja"), 2) == 0
    near1 = jnp.where(even, NJ - 1, 0)
    far1 = jnp.where(even, NJ - 2, 1)
    near2 = jnp.where(even, 0, NJ - 1)
    far2 = jnp.where(even, 1, NJ - 2)
    rows = ((p1_ref, near1, far1), (p2_ref, near2, far2))

    def windows(blocks, k, window):
        out = pltpu.roll(blocks[0], k, 1)
        for b in range(1, NB):
            out = jnp.where(window == b, pltpu.roll(blocks[b], b * 16 + k, 1), out)
        return out

    early[0].wait()
    place = (lane + 3) & (NI - 1)
    floor = windows([k_ref[pl.ds(8 * b, 8), :].astype(F32) for b in range(NB)], 0, lax.shift_right_logical(place, 4))
    first = (lane & 15) == 0
    k_cols = []
    for n, off in enumerate(COLS):
        x = jnp.where(first, pltpu.roll(floor, -off % NI, 1), 0.0)
        for step in (1, 2, 4, 8):
            x = x + pltpu.roll(x, step, 1)
        k_cols.append(x)
    early[1].wait()
    for ref, near, far in rows:
        for k in range(NK):
            ref[pl.ds(64 + k, 1), :] = v_ref[k, pl.ds(near, 1), :]
        ref[pl.ds(80, 8), :] = jnp.zeros((8, NI), F32)
        ref[pl.ds(80, 1), :] = k_ref[pl.ds(near, 1), :].astype(F32)
        ref[pl.ds(81, 1), :] = k_ref[pl.ds(far, 1), :].astype(F32)

    t_acc = [None] * 6
    s_acc = [None] * 6
    u_acc = [None] * 6
    for k in range(NK):
        if k % per == 0:
            for c in copies[k // per * 3 : k // per * 3 + 3]:
                c.wait()
        place = (lane - (k - 3)) & (NI - 1)
        window = lax.shift_right_logical(place, 4)
        within = place & 15
        for ref, acc, which in ((t_ref, t_acc, range(6)), (s_ref, s_acc, range(6)), (u_ref, u_acc, (1, 2, 3))):
            got = windows([ref[k, pl.ds(8 * b, 8), :] for b in range(NB)], k, window)
            for n in which:
                acc[n] = got if k == 0 else jnp.where(within == n, got, acc[n])
        for ref, near, far in rows:
            ref[pl.ds(k, 1), :] = t_ref[k, pl.ds(near, 1), :]
            ref[pl.ds(16 + k, 1), :] = t_ref[k, pl.ds(far, 1), :]
            ref[pl.ds(32 + k, 1), :] = s_ref[k, pl.ds(near, 1), :]
            ref[pl.ds(48 + k, 1), :] = s_ref[k, pl.ds(far, 1), :]
    t_cols = [pltpu.roll(x, -off % NI, 1) for x, off in zip(t_acc, COLS)]
    s_cols = [pltpu.roll(x, -off % NI, 1) for x, off in zip(s_acc, COLS)]
    u_cols = [pltpu.roll(u_acc[n], -COLS[n] % NI, 1) for n in (1, 2, 3)]
    for n, x in enumerate(t_cols + s_cols + k_cols + u_cols):
        own_ref[n] = x
    for n, x in enumerate((t_cols[2], t_cols[1], s_cols[2], s_cols[1], k_cols[2], k_cols[1], u_cols[1])):
        east_ref[n] = x
    for n, x in enumerate((t_cols[3], t_cols[4], s_cols[3], s_cols[4], k_cols[3], k_cols[4])):
        west_ref[n] = x

    @pl.when(bulk_first())
    def _():
        bulk_fluxes(t_ref, s_ref, u_ref, v_ref, w_hbm, k_ref, ts_ref, ss_ref, *scratch)


def pack(t, s, u, v, w, floor):
    fields = [pltpu.with_memory_space_constraint(x, pltpu.HBM) for x in (t, s, u, v, w, floor)]
    return pl.pallas_call(
        pack_kernel,
        out_shape=tuple(
            pltpu.VMEM(shape, F32) for shape in ((MROWS, NI), (11, 8, NI), (11, 8, NI), (MROWS, NI), (21, 8, NI))
        )
        + (pltpu.VMEM((NK, NJ, NI), F32),) * 4
        + (pltpu.VMEM((NJ, NI), jnp.int32),)
        + (pltpu.VMEM((NK, NJ, NI), F32),) * 2,
        in_specs=[pl.BlockSpec(memory_space=pltpu.HBM)] * 6,
        out_specs=(pl.BlockSpec(memory_space=pltpu.VMEM),) * 12,
        scratch_shapes=[pltpu.SemaphoreType.DMA((14,))] + bulk_scratch(),
        compiler_params=pltpu.CompilerParams(vmem_limit_bytes=16 * 2**20),
        name="pack_edges",
    )(*fields)


def edge_fluxes(level, q, floor, c):
    is_open = [level < jnp.minimum(a, b) for a, b in zip(floor, floor[1:])]
    g = [jnp.where(o, b - a, 0.0) for o, a, b in zip(is_open, q, q[1:])]
    slope = [None] + [minmod(a, b) for a, b in zip(g, g[1:])]
    out = []
    for n, x in zip((1, 2), c):
        out.append(flux(x, jnp.where(is_open[n], x, 0.0), slope_factor(x), q[n], slope[n], q[n + 1], slope[n + 1]))
    return out


def solve_kernel(
    t_ref, s_ref, u_ref, v_ref, w_hbm, k_ref, ts_in, ss_in, own_ref,
    p2_ref, east_ref, west_ref, p1_ref, tn_hbm, sn_hbm,
    ts_ref, ss_ref, to_ref, so_ref, zonal_ref, merid_ref, rows_ref, out_sems, *scratch,
):
    done_first = bulk_first()

    @pl.when(jnp.logical_not(done_first))
    def _():
        bulk_fluxes(t_ref, s_ref, u_ref, v_ref, w_hbm, k_ref, ts_ref, ss_ref, *scratch)

    for k in range(NK):
        for n, r in enumerate(ROWS):
            rows_ref[n, pl.ds(k, 1), :] = t_ref[k, pl.ds(r, 1), :]
            rows_ref[6 + n, pl.ds(k, 1), :] = s_ref[k, pl.ds(r, 1), :]
        for n, r in enumerate((0, 62, 63)):
            rows_ref[12 + n, pl.ds(k, 1), :] = v_ref[k, pl.ds(r, 1), :]

    lane = lanes()
    ja = lax.axis_index("ja")
    even = lax.rem(ja, 2) == 0
    is_north = ja == lax.axis_size("ja") - 1

    level = (lane & 15).astype(F32)
    own = [own_ref[n] for n in range(21)]
    k_own = own[12:18]
    u_own = own[18:21]
    west_floor = [east_ref[5], east_ref[4]] + k_own[3:6]
    east_floor = k_own[0:3] + [west_ref[4], west_ref[5]]
    for n in range(2):
        q = own[6 * n : 6 * n + 6]
        f0, f1 = edge_fluxes(level, [east_ref[2 * n + 1], east_ref[2 * n]] + q[3:6], west_floor, (east_ref[6], u_own[2]))
        f2, f3 = edge_fluxes(level, q[0:3] + [west_ref[2 * n], west_ref[2 * n + 1]], east_floor, (u_own[0], u_own[1]))
        parts = (f2, f3 - f2, f1 - f0, -f1)
        for r in range(4):
            x = parts[0] if r == 0 else pltpu.roll(parts[0], (0 - r) % NI, 1)
            for i in range(1, 4):
                moved = parts[i] if i == r else pltpu.roll(parts[i], (i - r) % NI, 1)
                x = jnp.where((lane & 3) == i, moved, x)
            zonal_ref[n, r] = x

    level = lax.broadcasted_iota(jnp.int32, (NK, NI), 0).astype(F32)
    turned = NI - 1 - lanes()
    p1 = [p1_ref[pl.ds(8 * n, 8), :] for n in range(MROWS // 8)]
    p2 = [p2_ref[pl.ds(8 * n, 8), :] for n in range(MROWS // 8)]
    south = [jnp.where(even, b, a) for a, b in zip(p1, p2)]
    north = [jnp.where(is_north, jnp.take_along_axis(b, turned, axis=1), jnp.where(even, a, b)) for a, b in zip(p1, p2)]

    def plane(msg, n):
        return jnp.concatenate([msg[2 * n], msg[2 * n + 1]], axis=0)

    def wide(row):
        return jnp.broadcast_to(row, (NK, NI))

    floors = [wide(k_ref[pl.ds(r, 1), :].astype(F32)) for r in ROWS]
    s_floor = [wide(south[10][1:2]), wide(south[10][0:1])] + floors[0:3]
    n_floor = floors[3:6] + [wide(north[10][0:1]), wide(north[10][1:2])]
    last = jnp.where(is_north, 0.5 * (rows_ref[14] - plane(north, 4)), rows_ref[14])
    merid_ref[...] = jnp.zeros_like(merid_ref)
    for n in range(2):
        q = [rows_ref[6 * n + r] for r in range(6)]
        f0, f1 = edge_fluxes(level, [plane(south, 2 * n + 1), plane(south, 2 * n)] + q[0:3], s_floor, (plane(south, 4), rows_ref[12]))
        f2, f3 = edge_fluxes(level, q[3:6] + [plane(north, 2 * n), plane(north, 2 * n + 1)], n_floor, (rows_ref[13], last))
        for side, r, x in ((0, 0, f1 - f0), (0, 1, -f1), (2, 6, f2), (2, 7, f3 - f2)):
            for k in range(NK):
                merid_ref[n, side, k, pl.ds(r, 1), :] = x[k : k + 1]

    edge_lanes = (lane < 2) | (lane >= NI - 2)

    def block(b):
        return pl.ds(pl.multiple_of(b * SOLVE_ROWS, SOLVE_ROWS), SOLVE_ROWS)

    def out_copies(b):
        at = block(b)
        return [
            pltpu.make_async_copy(to_ref.at[:, at], tn_hbm.at[:, at], out_sems.at[0, b]),
            pltpu.make_async_copy(so_ref.at[:, at], sn_hbm.at[:, at], out_sems.at[1, b]),
        ]

    def column(b, _):
        at = block(b)
        floor = k_ref[at, :]
        wet = [floor > k for k in range(NK)]
        star = []
        for n, (first, ref) in enumerate(((ts_in, ts_ref), (ss_in, ss_ref))):
            star.append([])
            for k in range(NK):
                corrections = []
                for h in range(SOLVE_ROWS // 8):
                    c = b * (SOLVE_ROWS // 8) + h
                    z = pltpu.roll(zonal_ref[n, k % 4], lax.rem(2 * NI - 2 - 4 * (k // 4) - 16 * c, NI), 1)
                    side = jnp.where(c == 0, 0, jnp.where(c == NB - 1, 2, 1))
                    corrections.append(jnp.where(edge_lanes, z, 0.0) + merid_ref[n, side, k])
                x = jnp.where(done_first, first[k, at, :], ref[k, at, :]) - jnp.concatenate(corrections, axis=0)
                star[n].append(jnp.where(wet[k], x, 0.0))
        dens = []
        for k in range(NK):
            z = LAYER_DEPTH * (k + 0.5)
            ta = star[0][k] - 10.0
            sa = star[1][k] - 35.0
            heat = (-0.5 * THERMAL_COEF * CABBELING_T) * ta - MIXED_COEF * sa - THERMAL_COEF * (1.0 + THERMOBARIC_T * z)
            salt = (-0.5 * HALINE_COEF * CABBELING_S) * sa + HALINE_COEF * (1.0 - THERMOBARIC_S * z)
            dens.append(heat * ta + salt * sa)
        above = None
        ratio = []
        values = ([], [])
        for k in range(NK):
            if k < NK - 1:
                below = jnp.where(wet[k + 1], 5.5 - 5.0 * jnp.tanh(dens[k + 1] - dens[k]), 0.0)
                pivot = 1.0 + below
            else:
                below = None
                pivot = 1.0
            if k > 0:
                pivot = pivot + above * (1.0 - ratio[-1])
            r = pl.reciprocal(pivot, approx=True)
            r = r * (2.0 - pivot * r)
            if below is not None:
                ratio.append(below * r)
            for n in range(2):
                x = star[n][k]
                if k > 0:
                    x = x + above * values[n][-1]
                values[n].append(x * r)
            above = below
        for n, out in enumerate((to_ref, so_ref)):
            x = values[n][NK - 1]
            out[NK - 1, at, :] = jnp.where(wet[NK - 1], x, 0.0)
            for k in range(NK - 2, -1, -1):
                x = values[n][k] + ratio[k] * x
                out[k, at, :] = jnp.where(wet[k], x, 0.0)
        for c in out_copies(b):
            c.start()
        return 0

    lax.fori_loop(0, NJ // SOLVE_ROWS, column, 0)
    for b in range(NJ // SOLVE_ROWS):
        for c in out_copies(b):
            c.wait()


def solve(t, s, u, v, w, floor, ts, ss, *edges):
    vmem = pl.BlockSpec(memory_space=pltpu.VMEM)
    hbm = pl.BlockSpec(memory_space=pltpu.HBM)
    field = pltpu.VMEM((NK, NJ, NI), F32)
    w = pltpu.with_memory_space_constraint(w, pltpu.HBM)
    return pl.pallas_call(
        solve_kernel,
        out_shape=(jax.ShapeDtypeStruct((NK, NJ, NI), F32),) * 2,
        in_specs=[vmem] * 4 + [hbm] + [vmem] * (3 + len(edges)),
        out_specs=(hbm, hbm),
        scratch_shapes=[field] * 4
        + [
            pltpu.VMEM((2, 4, 8, NI), F32),
            pltpu.VMEM((2, 3, NK, 8, NI), F32),
            pltpu.VMEM((15, NK, NI), F32),
            pltpu.SemaphoreType.DMA((2, NB)),
        ]
        + bulk_scratch(),
        compiler_params=pltpu.CompilerParams(vmem_limit_bytes=24 * 2**20),
        cost_estimate=pl.CostEstimate(flops=6_000_000, bytes_accessed=2_500_000, transcendentals=300_000),
        name="solve_columns",
    )(t, s, u, v, w, floor, ts, ss, *edges)


def local(nj, ni, t, s, u, v, w, floor):
    p2, east, west, p1, own, t, s, u, v, floor, ts, ss = pack(t, s, u, v, w, floor)
    first = []
    second = []
    for i in range(ni):
        for j in range(0, nj, 2):
            first += [(j * ni + i, (j + 1) * ni + i), ((j + 1) * ni + i, j * ni + i)]
        for j in range(1, nj - 1, 2):
            second += [(j * ni + i, (j + 1) * ni + i), ((j + 1) * ni + i, j * ni + i)]
        second.append(((nj - 1) * ni + i, (nj - 1) * ni + ni - 1 - i))
    p1 = lax.ppermute(p1, ("ja", "ia"), first)
    p2 = lax.ppermute(p2, ("ja", "ia"), second)
    from_west = lax.ppermute(east, "ia", [(i, (i + 1) % ni) for i in range(ni)])
    from_east = lax.ppermute(west, "ia", [((i + 1) % ni, i) for i in range(ni)])
    return solve(t, s, u, v, w, floor, ts, ss, own, p2, from_west, from_east, p1)


def solution(mesh):
    field = P(None, "ja", "ia")
    return jax.shard_map(
        functools.partial(local, mesh.shape["ja"], mesh.shape["ia"]),
        mesh=mesh,
        in_specs=(field,) * 5 + (P("ja", "ia"),),
        out_specs=(field, field),
        check_vma=False,
    )
```

```python
import functools

import jax
import jax.numpy as jnp
from jax import lax
from jax.experimental import pallas as pl
from jax.experimental.pallas import tpu as pltpu
from jax.sharding import PartitionSpec as P

THERMAL_COEF = 0.1655
HALINE_COEF = 0.76554
CABBELING_T = 0.05952
CABBELING_S = 0.00054914
THERMOBARIC_T = 0.0001497
THERMOBARIC_S = 1.109e-05
MIXED_COEF = 0.0024341
LAYER_DEPTH = 50.0

NK = 16
NJ = 64
NI = 128
NB = NJ // 8
HALF = NJ // 2
F32 = jnp.float32

COLS = (-3, -2, -1, 0, 1, 2)
MROWS = 88


def lanes():
    return lax.broadcasted_iota(jnp.int32, (8, NI), 1)


def sublanes():
    return lax.broadcasted_iota(jnp.int32, (8, NI), 0)


def minmod(x, y):
    return jnp.maximum(jnp.minimum(x, jnp.maximum(y, 0.0)), jnp.minimum(y, 0.0))


def slope_factor(c):
    return jnp.where(c > 0, 0.5, -0.5) - 0.5 * c


def flux(c, c_open, factor, qa, sa, qb, sb):
    up = c > 0
    return c_open * (jnp.where(up, qa, qb) + factor * jnp.where(up, sa, sb))


def bulk_fluxes(t_ref, s_ref, u_ref, v_ref, w_hbm, k_ref, to_ref, so_ref, w_ref, th_ref, sh_ref, mask_ref, sem):
    w_copy = pltpu.make_async_copy(w_hbm, w_ref, sem)
    w_copy.start()
    lane = lanes()
    sub = sublanes()
    floors = [k_ref[pl.ds(m, 8, stride=8), :] for m in range(NB)]
    for m in range(NB):
        east = jnp.where(lane == NI - 1, 0, jnp.minimum(floors[m], pltpu.roll(floors[m], NI - 1, 1)))
        if m < NB - 1:
            north = jnp.minimum(floors[m], floors[m + 1])
        else:
            north = jnp.where(sub == 7, 0, jnp.minimum(floors[m], pltpu.roll(floors[0], 7, 0)))
        mask_ref[0, m] = east
        mask_ref[1, m] = jnp.where((lane == 0) | (lane == NI - 2), 0, east)
        mask_ref[2, m] = north
        inner = north
        if m == 0:
            inner = jnp.where(sub == 0, 0, inner)
        if m == NB - 2:
            inner = jnp.where(sub == 7, 0, inner)
        mask_ref[3, m] = inner

    def level(k):
        q = [[ref[k, pl.ds(m, 8, stride=8), :] for m in range(NB)] for ref in (t_ref, s_ref)]
        c = [v_ref[k, pl.ds(m, 8, stride=8), :] for m in range(NB)]
        c_open = [jnp.where(mask_ref[3, m] > k, c[m], 0.0) for m in range(NB)]
        is_open = [mask_ref[2, m] > k for m in range(NB)]
        factor = [slope_factor(x) for x in c]
        left = []
        for x in q:
            after = x[1:] + [pltpu.roll(x[0], 7, 0)]
            g = [jnp.where(o, b - a, 0.0) for o, a, b in zip(is_open, x, after)]
            g_before = [pltpu.roll(g[-1], 1, 0)] + g[:-1]
            slope = [minmod(a, b) for a, b in zip(g, g_before)]
            slope_after = slope[1:] + [pltpu.roll(slope[0], 7, 0)]
            f = [flux(*y) for y in zip(c, c_open, factor, x, slope, after, slope_after)]
            f_before = [pltpu.roll(f[-1], 1, 0)] + f[:-1]
            left.append([a - (b - d) for a, b, d in zip(x, f, f_before)])
        for m in range(NB):
            c = u_ref[k, pl.ds(m, 8, stride=8), :]
            c_open = jnp.where(mask_ref[1, m] > k, c, 0.0)
            is_open = mask_ref[0, m] > k
            factor = slope_factor(c)
            for n, out in ((0, th_ref), (1, sh_ref)):
                x = q[n][m]
                after = pltpu.roll(x, NI - 1, 1)
                g = jnp.where(is_open, after - x, 0.0)
                slope = minmod(g, pltpu.roll(g, 1, 1))
                f = flux(c, c_open, factor, x, slope, after, pltpu.roll(slope, NI - 1, 1))
                out[k, pl.ds(m, 8, stride=8), :] = left[n][m] - (f - pltpu.roll(f, 1, 1))

    @pl.loop(0, NK, unroll=4)
    def _(k):
        level(k)

    w_copy.wait()

    def column(b, _):
        at = pl.ds(pl.multiple_of(b * 8, 8), 8)
        floor = k_ref[at, :]
        c = [w_ref[k, at, :] for k in range(NK - 1)]
        is_open = [floor > k + 1 for k in range(NK - 1)]
        c_open = [jnp.where(o, x, 0.0) for o, x in zip(is_open, c)]
        factor = [slope_factor(x) for x in c]
        for src, half, out in ((t_ref, th_ref, to_ref), (s_ref, sh_ref, so_ref)):
            x = [src[k, at, :] for k in range(NK)]
            g = [jnp.where(is_open[k], x[k + 1] - x[k], 0.0) for k in range(NK - 1)]
            slope = [jnp.zeros((8, NI), F32)] + [minmod(g[k], g[k - 1]) for k in range(1, NK - 1)] + [jnp.zeros((8, NI), F32)]
            before = None
            for k in range(NK):
                y = half[k, at, :]
                if k < NK - 1:
                    f = flux(c[k], c_open[k], factor[k], x[k], slope[k], x[k + 1], slope[k + 1])
                    y = y - (f if before is None else f - before)
                    before = f
                else:
                    y = y + before
                out[k, at, :] = y
        return 0

    lax.fori_loop(0, NB, column, 0)


def bulk_scratch():
    field = pltpu.VMEM((NK, NJ, NI), F32)
    return [field, field, field, pltpu.VMEM((4, NB, 8, NI), jnp.int32), pltpu.SemaphoreType.DMA(())]


def bulk_first():
    ja, ia = lax.axis_index("ja"), lax.axis_index("ia")
    ni = lax.axis_size("ia")
    near_fold = ja >= lax.axis_size("ja") - 2
    return ia < jnp.where(near_fold, 3 * ni // 8, ni // 8)


def pack_kernel(
    t_hbm, s_hbm, u_hbm, v_hbm, w_hbm, k_hbm, p2_ref, east_ref, west_ref, p1_ref, own_ref,
    t_ref, s_ref, u_ref, v_ref, k_ref, ts_ref, ss_ref, sems, *scratch,
):
    chunks = 4
    per = NK // chunks
    copies = []
    for c in range(chunks):
        part = pl.ds(c * per, per)
        for f, (src, dst) in enumerate(((t_hbm, t_ref), (s_hbm, s_ref), (u_hbm, u_ref))):
            copies.append(pltpu.make_async_copy(src.at[part], dst.at[part], sems.at[c * 3 + f]))
    early = [
        pltpu.make_async_copy(k_hbm, k_ref, sems.at[12]),
        pltpu.make_async_copy(v_hbm, v_ref, sems.at[13]),
    ]
    for c in early + copies:
        c.start()

    lane = lanes()
    even = lax.rem(lax.axis_index("ja"), 2) == 0
    near1 = jnp.where(even, NJ - 1, 0)
    far1 = jnp.where(even, NJ - 2, 1)
    near2 = jnp.where(even, 0, NJ - 1)
    far2 = jnp.where(even, 1, NJ - 2)
    rows = ((p1_ref, near1, far1), (p2_ref, near2, far2))

    def windows(blocks, k, window):
        out = pltpu.roll(blocks[0], k, 1)
        for b in range(1, NB):
            out = jnp.where(window == b, pltpu.roll(blocks[b], b * 16 + k, 1), out)
        return out

    early[0].wait()
    place = (lane + 3) & (NI - 1)
    floor = windows([k_ref[pl.ds(8 * b, 8), :].astype(F32) for b in range(NB)], 0, lax.shift_right_logical(place, 4))
    first = (lane & 15) == 0
    k_cols = []
    for n, off in enumerate(COLS):
        x = jnp.where(first, pltpu.roll(floor, -off % NI, 1), 0.0)
        for step in (1, 2, 4, 8):
            x = x + pltpu.roll(x, step, 1)
        k_cols.append(x)
    early[1].wait()
    for ref, near, far in rows:
        for k in range(NK):
            ref[pl.ds(64 + k, 1), :] = v_ref[k, pl.ds(near, 1), :]
        ref[pl.ds(80, 8), :] = jnp.zeros((8, NI), F32)
        ref[pl.ds(80, 1), :] = k_ref[pl.ds(near, 1), :].astype(F32)
        ref[pl.ds(81, 1), :] = k_ref[pl.ds(far, 1), :].astype(F32)

    t_acc = [None] * 6
    s_acc = [None] * 6
    u_acc = [None] * 6
    for k in range(NK):
        if k % per == 0:
            for c in copies[k // per * 3 : k // per * 3 + 3]:
                c.wait()
        place = (lane - (k - 3)) & (NI - 1)
        window = lax.shift_right_logical(place, 4)
        within = place & 15
        for ref, acc, which in ((t_ref, t_acc, range(6)), (s_ref, s_acc, range(6)), (u_ref, u_acc, (1, 2, 3))):
            got = windows([ref[k, pl.ds(8 * b, 8), :] for b in range(NB)], k, window)
            for n in which:
                acc[n] = got if k == 0 else jnp.where(within == n, got, acc[n])
        for ref, near, far in rows:
            ref[pl.ds(k, 1), :] = t_ref[k, pl.ds(near, 1), :]
            ref[pl.ds(16 + k, 1), :] = t_ref[k, pl.ds(far, 1), :]
            ref[pl.ds(32 + k, 1), :] = s_ref[k, pl.ds(near, 1), :]
            ref[pl.ds(48 + k, 1), :] = s_ref[k, pl.ds(far, 1), :]
    t_cols = [pltpu.roll(x, -off % NI, 1) for x, off in zip(t_acc, COLS)]
    s_cols = [pltpu.roll(x, -off % NI, 1) for x, off in zip(s_acc, COLS)]
    u_cols = [pltpu.roll(u_acc[n], -COLS[n] % NI, 1) for n in (1, 2, 3)]
    for n, x in enumerate(t_cols + s_cols + k_cols + u_cols):
        own_ref[n] = x
    for n, x in enumerate((t_cols[2], t_cols[1], s_cols[2], s_cols[1], k_cols[2], k_cols[1], u_cols[1])):
        east_ref[n] = x
    for n, x in enumerate((t_cols[3], t_cols[4], s_cols[3], s_cols[4], k_cols[3], k_cols[4])):
        west_ref[n] = x

    @pl.when(bulk_first())
    def _():
        bulk_fluxes(t_ref, s_ref, u_ref, v_ref, w_hbm, k_ref, ts_ref, ss_ref, *scratch)


def pack(t, s, u, v, w, floor):
    fields = [pltpu.with_memory_space_constraint(x, pltpu.HBM) for x in (t, s, u, v, w, floor)]
    return pl.pallas_call(
        pack_kernel,
        out_shape=tuple(
            pltpu.VMEM(shape, F32) for shape in ((MROWS, NI), (11, 8, NI), (11, 8, NI), (MROWS, NI), (21, 8, NI))
        )
        + (pltpu.VMEM((NK, NJ, NI), F32),) * 4
        + (pltpu.VMEM((NJ, NI), jnp.int32),)
        + (pltpu.VMEM((NK, NJ, NI), F32),) * 2,
        in_specs=[pl.BlockSpec(memory_space=pltpu.HBM)] * 6,
        out_specs=(pl.BlockSpec(memory_space=pltpu.VMEM),) * 12,
        scratch_shapes=[pltpu.SemaphoreType.DMA((14,))] + bulk_scratch(),
        compiler_params=pltpu.CompilerParams(vmem_limit_bytes=16 * 2**20),
        name="pack_edges",
    )(*fields)


def edge_fluxes(level, q, floor, c):
    is_open = [level < jnp.minimum(a, b) for a, b in zip(floor, floor[1:])]
    g = [jnp.where(o, b - a, 0.0) for o, a, b in zip(is_open, q, q[1:])]
    slope = [None] + [minmod(a, b) for a, b in zip(g, g[1:])]
    out = []
    for n, x in zip((1, 2), c):
        out.append(flux(x, jnp.where(is_open[n], x, 0.0), slope_factor(x), q[n], slope[n], q[n + 1], slope[n + 1]))
    return out


def solve_rows(south, folded, t_ref, s_ref, v_ref, k_ref, msg_ref, zonal_ref, stars, outs, rows_ref, merid_ref):
    lane = lanes()
    base = jnp.where(south, 0, NJ - 3)
    for k in range(NK):
        for n, ref in enumerate((t_ref, s_ref, v_ref)):
            for r in range(3):
                rows_ref[3 * n + r, pl.ds(k, 1), :] = ref[k, pl.ds(base + r, 1), :]

    level = lax.broadcasted_iota(jnp.int32, (NK, NI), 0).astype(F32)
    msg = [msg_ref[pl.ds(8 * n, 8), :] for n in range(MROWS // 8)]
    if folded is not None:
        turned = NI - 1 - lane
        msg = [jnp.where(folded, jnp.take_along_axis(x, turned, axis=1), x) for x in msg]

    def plane(n):
        return jnp.concatenate([msg[2 * n], msg[2 * n + 1]], axis=0)

    def wide(row):
        return jnp.broadcast_to(row, (NK, NI))

    def in_order(own, near, far):
        return [jnp.where(south, x, y) for x, y in zip([far, near] + own, own + [near, far])]

    floors = in_order([wide(k_ref[pl.ds(base + r, 1), :].astype(F32)) for r in range(3)], wide(msg[10][0:1]), wide(msg[10][1:2]))
    last = rows_ref[8]
    if folded is not None:
        last = jnp.where(folded, 0.5 * (last - plane(4)), last)
    courant = (jnp.where(south, plane(4), rows_ref[7]), jnp.where(south, rows_ref[6], last))
    merid_ref[...] = jnp.zeros_like(merid_ref)
    at_row = jnp.where(south, 0, 6)
    for n in range(2):
        q = in_order([rows_ref[3 * n + r] for r in range(3)], plane(2 * n), plane(2 * n + 1))
        f0, f1 = edge_fluxes(level, q, floors, courant)
        for i, x in enumerate((jnp.where(south, f1 - f0, f0), jnp.where(south, -f1, f1 - f0))):
            for k in range(NK):
                merid_ref[n, k, pl.ds(at_row + i, 1), :] = x[k : k + 1]

    edge_lanes = (lane < 2) | (lane >= NI - 2)
    half = jnp.where(south, 0, 1)
    at = half_rows(south)
    floor = k_ref[at, :]
    wet = [floor > k for k in range(NK)]
    star = []
    for n in range(2):
        star.append([])
        for k in range(NK):
            corrections = []
            for h in range(HALF // 8):
                c = half * (HALF // 8) + h
                z = pltpu.roll(zonal_ref[n, k % 4], lax.rem(2 * NI - 2 - 4 * (k // 4) - 16 * c, NI), 1)
                z = jnp.where(edge_lanes, z, 0.0)
                if h == 0:
                    z = z + jnp.where(south, merid_ref[n, k], 0.0)
                if h == HALF // 8 - 1:
                    z = z + jnp.where(south, 0.0, merid_ref[n, k])
                corrections.append(z)
            star[n].append(jnp.where(wet[k], stars(n, k, at) - jnp.concatenate(corrections, axis=0), 0.0))
    dens = []
    for k in range(NK):
        z = LAYER_DEPTH * (k + 0.5)
        ta = star[0][k] - 10.0
        sa = star[1][k] - 35.0
        heat = (-0.5 * THERMAL_COEF * CABBELING_T) * ta - MIXED_COEF * sa - THERMAL_COEF * (1.0 + THERMOBARIC_T * z)
        salt = (-0.5 * HALINE_COEF * CABBELING_S) * sa + HALINE_COEF * (1.0 - THERMOBARIC_S * z)
        dens.append(heat * ta + salt * sa)
    above = None
    ratio = []
    values = ([], [])
    for k in range(NK):
        if k < NK - 1:
            below = jnp.where(wet[k + 1], 5.5 - 5.0 * jnp.tanh(dens[k + 1] - dens[k]), 0.0)
            pivot = 1.0 + below
        else:
            below = None
            pivot = 1.0
        if k > 0:
            pivot = pivot + above * (1.0 - ratio[-1])
        r = pl.reciprocal(pivot, approx=True)
        r = r * (2.0 - pivot * r)
        if below is not None:
            ratio.append(below * r)
        for n in range(2):
            x = star[n][k]
            if k > 0:
                x = x + above * values[n][-1]
            values[n].append(x * r)
        above = below
    for n in range(2):
        x = values[n][NK - 1]
        outs[n][NK - 1] = jnp.where(wet[NK - 1], x, 0.0)
        for k in range(NK - 2, -1, -1):
            x = values[n][k] + ratio[k] * x
            outs[n][k] = jnp.where(wet[k], x, 0.0)


def half_rows(south):
    return pl.ds(pl.multiple_of(jnp.where(south, 0, HALF), HALF), HALF)


def even_row():
    return lax.rem(lax.axis_index("ja"), 2) == 0


def first_kernel(
    t_ref, s_ref, u_ref, v_ref, w_hbm, k_ref, ts_in, ss_in, own_ref, east_ref, p2_ref, west_ref,
    tn_ref, sn_ref, ts_ref, ss_ref, zonal_ref, rows_ref, merid_ref, *scratch,
):
    done_first = bulk_first()

    @pl.when(jnp.logical_not(done_first))
    def _():
        bulk_fluxes(t_ref, s_ref, u_ref, v_ref, w_hbm, k_ref, ts_ref, ss_ref, *scratch)

    lane = lanes()
    level = (lane & 15).astype(F32)
    own = [own_ref[n] for n in range(21)]
    k_own = own[12:18]
    u_own = own[18:21]
    west_floor = [east_ref[5], east_ref[4]] + k_own[3:6]
    east_floor = k_own[0:3] + [west_ref[4], west_ref[5]]
    for n in range(2):
        q = own[6 * n : 6 * n + 6]
        f0, f1 = edge_fluxes(level, [east_ref[2 * n + 1], east_ref[2 * n]] + q[3:6], west_floor, (east_ref[6], u_own[2]))
        f2, f3 = edge_fluxes(level, q[0:3] + [west_ref[2 * n], west_ref[2 * n + 1]], east_floor, (u_own[0], u_own[1]))
        parts = (f2, f3 - f2, f1 - f0, -f1)
        for r in range(4):
            x = parts[0] if r == 0 else pltpu.roll(parts[0], (0 - r) % NI, 1)
            for i in range(1, 4):
                moved = parts[i] if i == r else pltpu.roll(parts[i], (i - r) % NI, 1)
                x = jnp.where((lane & 3) == i, moved, x)
            zonal_ref[n, r] = x

    def stars(n, k, at):
        return jnp.where(done_first, (ts_in, ss_in)[n][k, at, :], (ts_ref, ss_ref)[n][k, at, :])

    folded = lax.axis_index("ja") == lax.axis_size("ja") - 1
    solve_rows(even_row(), folded, t_ref, s_ref, v_ref, k_ref, p2_ref, zonal_ref, stars, (tn_ref, sn_ref), rows_ref, merid_ref)


def first_half(t, s, u, v, w, floor, ts, ss, *edges):
    vmem = pl.BlockSpec(memory_space=pltpu.VMEM)
    hbm = pl.BlockSpec(memory_space=pltpu.HBM)
    w = pltpu.with_memory_space_constraint(w, pltpu.HBM)
    return pl.pallas_call(
        first_kernel,
        out_shape=(pltpu.VMEM((NK, HALF, NI), F32),) * 2
        + (pltpu.VMEM((NK, NJ, NI), F32),) * 2
        + (pltpu.VMEM((2, 4, 8, NI), F32),),
        in_specs=[vmem] * 4 + [hbm] + [vmem] * (3 + len(edges)),
        out_specs=(vmem,) * 5,
        scratch_shapes=[pltpu.VMEM((9, NK, NI), F32), pltpu.VMEM((2, NK, 8, NI), F32)] + bulk_scratch(),
        compiler_params=pltpu.CompilerParams(vmem_limit_bytes=24 * 2**20),
        cost_estimate=pl.CostEstimate(flops=16_000_000, bytes_accessed=4_000_000, transcendentals=150_000),
        name="solve_first_half",
    )(t, s, u, v, w, floor, ts, ss, *edges)


def second_kernel(
    t_ref, s_ref, v_ref, k_ref, ts_in, ss_in, ts_late, ss_late, zonal_ref, tn_ref, sn_ref, p1_ref, tn_hbm, sn_hbm,
    to_ref, so_ref, rows_ref, merid_ref, sems,
):
    south = jnp.logical_not(even_row())
    other, mine = half_rows(jnp.logical_not(south)), half_rows(south)
    first = [pltpu.make_async_copy(tn_ref, tn_hbm.at[:, other], sems.at[0]), pltpu.make_async_copy(sn_ref, sn_hbm.at[:, other], sems.at[1])]
    for c in first:
        c.start()
    done_first = bulk_first()

    def stars(n, k, at):
        return jnp.where(done_first, (ts_in, ss_in)[n][k, at, :], (ts_late, ss_late)[n][k, at, :])

    solve_rows(south, None, t_ref, s_ref, v_ref, k_ref, p1_ref, zonal_ref, stars, (to_ref, so_ref), rows_ref, merid_ref)
    second = [pltpu.make_async_copy(to_ref, tn_hbm.at[:, mine], sems.at[2]), pltpu.make_async_copy(so_ref, sn_hbm.at[:, mine], sems.at[3])]
    for c in second:
        c.start()
    for c in first + second:
        c.wait()


def second_half(*operands):
    vmem = pl.BlockSpec(memory_space=pltpu.VMEM)
    hbm = pl.BlockSpec(memory_space=pltpu.HBM)
    half = pltpu.VMEM((NK, HALF, NI), F32)
    return pl.pallas_call(
        second_kernel,
        out_shape=(jax.ShapeDtypeStruct((NK, NJ, NI), F32),) * 2,
        in_specs=[vmem] * len(operands),
        out_specs=(hbm, hbm),
        scratch_shapes=[
            half,
            half,
            pltpu.VMEM((9, NK, NI), F32),
            pltpu.VMEM((2, NK, 8, NI), F32),
            pltpu.SemaphoreType.DMA((4,)),
        ],
        compiler_params=pltpu.CompilerParams(vmem_limit_bytes=24 * 2**20),
        cost_estimate=pl.CostEstimate(flops=3_000_000, bytes_accessed=2_000_000, transcendentals=150_000),
        name="solve_second_half",
    )(*operands)


def local(nj, ni, t, s, u, v, w, floor):
    p2, east, west, p1, own, t, s, u, v, floor, ts, ss = pack(t, s, u, v, w, floor)
    first = []
    second = []
    for i in range(ni):
        for j in range(0, nj, 2):
            first += [(j * ni + i, (j + 1) * ni + i), ((j + 1) * ni + i, j * ni + i)]
        for j in range(1, nj - 1, 2):
            second += [(j * ni + i, (j + 1) * ni + i), ((j + 1) * ni + i, j * ni + i)]
        second.append(((nj - 1) * ni + i, (nj - 1) * ni + ni - 1 - i))
    p1 = lax.ppermute(p1, ("ja", "ia"), first)
    p2 = lax.ppermute(p2, ("ja", "ia"), second)
    from_west = lax.ppermute(east, "ia", [(i, (i + 1) % ni) for i in range(ni)])
    from_east = lax.ppermute(west, "ia", [((i + 1) % ni, i) for i in range(ni)])
    tn, sn, ts_late, ss_late, zonal = first_half(t, s, u, v, w, floor, ts, ss, own, from_west, p2, from_east)
    return second_half(t, s, v, floor, ts, ss, ts_late, ss_late, zonal, tn, sn, p1)


def solution(mesh):
    field = P(None, "ja", "ia")
    return jax.shard_map(
        functools.partial(local, mesh.shape["ja"], mesh.shape["ia"]),
        mesh=mesh,
        in_specs=(field,) * 5 + (P("ja", "ia"),),
        out_specs=(field, field),
        check_vma=False,
    )
```

```python
import functools

import jax
import jax.numpy as jnp
from jax import lax
from jax.experimental import pallas as pl
from jax.experimental.pallas import tpu as pltpu
from jax.sharding import PartitionSpec as P

THERMAL_COEF = 0.1655
HALINE_COEF = 0.76554
CABBELING_T = 0.05952
CABBELING_S = 0.00054914
THERMOBARIC_T = 0.0001497
THERMOBARIC_S = 1.109e-05
MIXED_COEF = 0.0024341
LAYER_DEPTH = 50.0

NK = 16
NJ = 64
NI = 128
NB = NJ // 8
EDGE = NJ // 2
LAST = 16
F32 = jnp.float32

COLS = (-3, -2, -1, 0, 1, 2)
MROWS = 88


def lanes():
    return lax.broadcasted_iota(jnp.int32, (8, NI), 1)


def sublanes():
    return lax.broadcasted_iota(jnp.int32, (8, NI), 0)


def minmod(x, y):
    return jnp.maximum(jnp.minimum(x, jnp.maximum(y, 0.0)), jnp.minimum(y, 0.0))


def slope_factor(c):
    return jnp.where(c > 0, 0.5, -0.5) - 0.5 * c


def flux(c, c_open, factor, qa, sa, qb, sb):
    up = c > 0
    return c_open * (jnp.where(up, qa, qb) + factor * jnp.where(up, sa, sb))


def bulk_fluxes(t_ref, s_ref, u_ref, v_ref, w_hbm, k_ref, to_ref, so_ref, w_ref, th_ref, sh_ref, mask_ref, sem):
    w_copy = pltpu.make_async_copy(w_hbm, w_ref, sem)
    w_copy.start()
    lane = lanes()
    sub = sublanes()
    floors = [k_ref[pl.ds(m, 8, stride=8), :] for m in range(NB)]
    for m in range(NB):
        east = jnp.where(lane == NI - 1, 0, jnp.minimum(floors[m], pltpu.roll(floors[m], NI - 1, 1)))
        if m < NB - 1:
            north = jnp.minimum(floors[m], floors[m + 1])
        else:
            north = jnp.where(sub == 7, 0, jnp.minimum(floors[m], pltpu.roll(floors[0], 7, 0)))
        mask_ref[0, m] = east
        mask_ref[1, m] = jnp.where((lane == 0) | (lane == NI - 2), 0, east)
        mask_ref[2, m] = north
        inner = north
        if m == 0:
            inner = jnp.where(sub == 0, 0, inner)
        if m == NB - 2:
            inner = jnp.where(sub == 7, 0, inner)
        mask_ref[3, m] = inner

    def level(k):
        q = [[ref[k, pl.ds(m, 8, stride=8), :] for m in range(NB)] for ref in (t_ref, s_ref)]
        c = [v_ref[k, pl.ds(m, 8, stride=8), :] for m in range(NB)]
        c_open = [jnp.where(mask_ref[3, m] > k, c[m], 0.0) for m in range(NB)]
        is_open = [mask_ref[2, m] > k for m in range(NB)]
        factor = [slope_factor(x) for x in c]
        left = []
        for x in q:
            after = x[1:] + [pltpu.roll(x[0], 7, 0)]
            g = [jnp.where(o, b - a, 0.0) for o, a, b in zip(is_open, x, after)]
            g_before = [pltpu.roll(g[-1], 1, 0)] + g[:-1]
            slope = [minmod(a, b) for a, b in zip(g, g_before)]
            slope_after = slope[1:] + [pltpu.roll(slope[0], 7, 0)]
            f = [flux(*y) for y in zip(c, c_open, factor, x, slope, after, slope_after)]
            f_before = [pltpu.roll(f[-1], 1, 0)] + f[:-1]
            left.append([a - (b - d) for a, b, d in zip(x, f, f_before)])
        for m in range(NB):
            c = u_ref[k, pl.ds(m, 8, stride=8), :]
            c_open = jnp.where(mask_ref[1, m] > k, c, 0.0)
            is_open = mask_ref[0, m] > k
            factor = slope_factor(c)
            for n, out in ((0, th_ref), (1, sh_ref)):
                x = q[n][m]
                after = pltpu.roll(x, NI - 1, 1)
                g = jnp.where(is_open, after - x, 0.0)
                slope = minmod(g, pltpu.roll(g, 1, 1))
                f = flux(c, c_open, factor, x, slope, after, pltpu.roll(slope, NI - 1, 1))
                out[k, pl.ds(m, 8, stride=8), :] = left[n][m] - (f - pltpu.roll(f, 1, 1))

    @pl.loop(0, NK, unroll=4)
    def _(k):
        level(k)

    w_copy.wait()

    def column(b, _):
        at = pl.ds(pl.multiple_of(b * 8, 8), 8)
        floor = k_ref[at, :]
        c = [w_ref[k, at, :] for k in range(NK - 1)]
        is_open = [floor > k + 1 for k in range(NK - 1)]
        c_open = [jnp.where(o, x, 0.0) for o, x in zip(is_open, c)]
        factor = [slope_factor(x) for x in c]
        for src, half, out in ((t_ref, th_ref, to_ref), (s_ref, sh_ref, so_ref)):
            x = [src[k, at, :] for k in range(NK)]
            g = [jnp.where(is_open[k], x[k + 1] - x[k], 0.0) for k in range(NK - 1)]
            slope = [jnp.zeros((8, NI), F32)] + [minmod(g[k], g[k - 1]) for k in range(1, NK - 1)] + [jnp.zeros((8, NI), F32)]
            before = None
            for k in range(NK):
                y = half[k, at, :]
                if k < NK - 1:
                    f = flux(c[k], c_open[k], factor[k], x[k], slope[k], x[k + 1], slope[k + 1])
                    y = y - (f if before is None else f - before)
                    before = f
                else:
                    y = y + before
                out[k, at, :] = y
        return 0

    lax.fori_loop(0, NB, column, 0)


def bulk_scratch():
    field = pltpu.VMEM((NK, NJ, NI), F32)
    return [field, field, field, pltpu.VMEM((4, NB, 8, NI), jnp.int32), pltpu.SemaphoreType.DMA(())]


def bulk_first():
    ja, ia = lax.axis_index("ja"), lax.axis_index("ia")
    ni = lax.axis_size("ia")
    near_fold = ja >= lax.axis_size("ja") - 2
    return ia < jnp.where(near_fold, 3 * ni // 8, ni // 8)


def pack_kernel(
    t_hbm, s_hbm, u_hbm, v_hbm, w_hbm, k_hbm, p2_ref, east_ref, west_ref, p1_ref, own_ref,
    t_ref, s_ref, u_ref, v_ref, k_ref, ts_ref, ss_ref, sems, *scratch,
):
    chunks = 4
    per = NK // chunks
    copies = []
    for c in range(chunks):
        part = pl.ds(c * per, per)
        for f, (src, dst) in enumerate(((t_hbm, t_ref), (s_hbm, s_ref), (u_hbm, u_ref))):
            copies.append(pltpu.make_async_copy(src.at[part], dst.at[part], sems.at[c * 3 + f]))
    early = [
        pltpu.make_async_copy(k_hbm, k_ref, sems.at[12]),
        pltpu.make_async_copy(v_hbm, v_ref, sems.at[13]),
    ]
    for c in early + copies:
        c.start()

    lane = lanes()
    even = lax.rem(lax.axis_index("ja"), 2) == 0
    near1 = jnp.where(even, NJ - 1, 0)
    far1 = jnp.where(even, NJ - 2, 1)
    near2 = jnp.where(even, 0, NJ - 1)
    far2 = jnp.where(even, 1, NJ - 2)
    rows = ((p1_ref, near1, far1), (p2_ref, near2, far2))

    def windows(blocks, k, window):
        out = pltpu.roll(blocks[0], k, 1)
        for b in range(1, NB):
            out = jnp.where(window == b, pltpu.roll(blocks[b], b * 16 + k, 1), out)
        return out

    early[0].wait()
    place = (lane + 3) & (NI - 1)
    floor = windows([k_ref[pl.ds(8 * b, 8), :].astype(F32) for b in range(NB)], 0, lax.shift_right_logical(place, 4))
    first = (lane & 15) == 0
    k_cols = []
    for n, off in enumerate(COLS):
        x = jnp.where(first, pltpu.roll(floor, -off % NI, 1), 0.0)
        for step in (1, 2, 4, 8):
            x = x + pltpu.roll(x, step, 1)
        k_cols.append(x)
    early[1].wait()
    for ref, near, far in rows:
        for k in range(NK):
            ref[pl.ds(64 + k, 1), :] = v_ref[k, pl.ds(near, 1), :]
        ref[pl.ds(80, 8), :] = jnp.zeros((8, NI), F32)
        ref[pl.ds(80, 1), :] = k_ref[pl.ds(near, 1), :].astype(F32)
        ref[pl.ds(81, 1), :] = k_ref[pl.ds(far, 1), :].astype(F32)

    t_acc = [None] * 6
    s_acc = [None] * 6
    u_acc = [None] * 6
    for k in range(NK):
        if k % per == 0:
            for c in copies[k // per * 3 : k // per * 3 + 3]:
                c.wait()
        place = (lane - (k - 3)) & (NI - 1)
        window = lax.shift_right_logical(place, 4)
        within = place & 15
        for ref, acc, which in ((t_ref, t_acc, range(6)), (s_ref, s_acc, range(6)), (u_ref, u_acc, (1, 2, 3))):
            got = windows([ref[k, pl.ds(8 * b, 8), :] for b in range(NB)], k, window)
            for n in which:
                acc[n] = got if k == 0 else jnp.where(within == n, got, acc[n])
        for ref, near, far in rows:
            ref[pl.ds(k, 1), :] = t_ref[k, pl.ds(near, 1), :]
            ref[pl.ds(16 + k, 1), :] = t_ref[k, pl.ds(far, 1), :]
            ref[pl.ds(32 + k, 1), :] = s_ref[k, pl.ds(near, 1), :]
            ref[pl.ds(48 + k, 1), :] = s_ref[k, pl.ds(far, 1), :]
    t_cols = [pltpu.roll(x, -off % NI, 1) for x, off in zip(t_acc, COLS)]
    s_cols = [pltpu.roll(x, -off % NI, 1) for x, off in zip(s_acc, COLS)]
    u_cols = [pltpu.roll(u_acc[n], -COLS[n] % NI, 1) for n in (1, 2, 3)]
    for n, x in enumerate(t_cols + s_cols + k_cols + u_cols):
        own_ref[n] = x
    for n, x in enumerate((t_cols[2], t_cols[1], s_cols[2], s_cols[1], k_cols[2], k_cols[1], u_cols[1])):
        east_ref[n] = x
    for n, x in enumerate((t_cols[3], t_cols[4], s_cols[3], s_cols[4], k_cols[3], k_cols[4])):
        west_ref[n] = x

    @pl.when(bulk_first())
    def _():
        bulk_fluxes(t_ref, s_ref, u_ref, v_ref, w_hbm, k_ref, ts_ref, ss_ref, *scratch)


def pack(t, s, u, v, w, floor):
    fields = [pltpu.with_memory_space_constraint(x, pltpu.HBM) for x in (t, s, u, v, w, floor)]
    return pl.pallas_call(
        pack_kernel,
        out_shape=tuple(
            pltpu.VMEM(shape, F32) for shape in ((MROWS, NI), (11, 8, NI), (11, 8, NI), (MROWS, NI), (21, 8, NI))
        )
        + (pltpu.VMEM((NK, NJ, NI), F32),) * 4
        + (pltpu.VMEM((NJ, NI), jnp.int32),)
        + (pltpu.VMEM((NK, NJ, NI), F32),) * 2,
        in_specs=[pl.BlockSpec(memory_space=pltpu.HBM)] * 6,
        out_specs=(pl.BlockSpec(memory_space=pltpu.VMEM),) * 12,
        scratch_shapes=[pltpu.SemaphoreType.DMA((14,))] + bulk_scratch(),
        compiler_params=pltpu.CompilerParams(vmem_limit_bytes=16 * 2**20),
        name="pack_edges",
    )(*fields)


def edge_fluxes(level, q, floor, c):
    is_open = [level < jnp.minimum(a, b) for a, b in zip(floor, floor[1:])]
    g = [jnp.where(o, b - a, 0.0) for o, a, b in zip(is_open, q, q[1:])]
    slope = [None] + [minmod(a, b) for a, b in zip(g, g[1:])]
    out = []
    for n, x in zip((1, 2), c):
        out.append(flux(x, jnp.where(is_open[n], x, 0.0), slope_factor(x), q[n], slope[n], q[n + 1], slope[n + 1]))
    return out


def edge_rows(south, folded, t_ref, s_ref, v_ref, k_ref, msg_ref, rows_ref, merid_ref):
    lane = lanes()
    base = jnp.where(south, 0, NJ - 3)
    for k in range(NK):
        for n, ref in enumerate((t_ref, s_ref, v_ref)):
            for r in range(3):
                rows_ref[3 * n + r, pl.ds(k, 1), :] = ref[k, pl.ds(base + r, 1), :]

    level = lax.broadcasted_iota(jnp.int32, (NK, NI), 0).astype(F32)
    msg = [msg_ref[pl.ds(8 * n, 8), :] for n in range(MROWS // 8)]
    if folded is not None:
        turned = NI - 1 - lane
        msg = [jnp.where(folded, jnp.take_along_axis(x, turned, axis=1), x) for x in msg]

    def plane(n):
        return jnp.concatenate([msg[2 * n], msg[2 * n + 1]], axis=0)

    def wide(row):
        return jnp.broadcast_to(row, (NK, NI))

    def in_order(own, near, far):
        return [jnp.where(south, x, y) for x, y in zip([far, near] + own, own + [near, far])]

    floors = in_order([wide(k_ref[pl.ds(base + r, 1), :].astype(F32)) for r in range(3)], wide(msg[10][0:1]), wide(msg[10][1:2]))
    last = rows_ref[8]
    if folded is not None:
        last = jnp.where(folded, 0.5 * (last - plane(4)), last)
    courant = (jnp.where(south, plane(4), rows_ref[7]), jnp.where(south, rows_ref[6], last))
    merid_ref[...] = jnp.zeros_like(merid_ref)
    at_row = jnp.where(south, 0, 6)
    for n in range(2):
        q = in_order([rows_ref[3 * n + r] for r in range(3)], plane(2 * n), plane(2 * n + 1))
        f0, f1 = edge_fluxes(level, q, floors, courant)
        for i, x in enumerate((jnp.where(south, f1 - f0, f0), jnp.where(south, -f1, f1 - f0))):
            for k in range(NK):
                merid_ref[n, k, pl.ds(at_row + i, 1), :] = x[k : k + 1]


def solve_rows(start, count, south, k_ref, zonal_ref, merid_ref, stars, outs, first_row):
    lane = lanes()
    edge_lanes = (lane < 2) | (lane >= NI - 2)
    at = pl.ds(pl.multiple_of(start, 8), count)
    to = pl.ds(pl.multiple_of(start - first_row, 8), count)
    floor = k_ref[at, :]
    wet = [floor > k for k in range(NK)]
    star = []
    for n in range(2):
        star.append([])
        for k in range(NK):
            corrections = []
            for h in range(count // 8):
                c = start // 8 + h
                z = pltpu.roll(zonal_ref[n, k % 4], lax.rem(2 * NI - 2 - 4 * (k // 4) - 16 * c, NI), 1)
                z = jnp.where(edge_lanes, z, 0.0)
                if merid_ref is not None and count == 8:
                    z = z + merid_ref[n, k]
                elif merid_ref is not None and h in (0, count // 8 - 1):
                    z = z + jnp.where(south if h == 0 else jnp.logical_not(south), merid_ref[n, k], 0.0)
                corrections.append(z)
            star[n].append(jnp.where(wet[k], stars(n, k, at) - jnp.concatenate(corrections, axis=0), 0.0))
    dens = []
    for k in range(NK):
        z = LAYER_DEPTH * (k + 0.5)
        ta = star[0][k] - 10.0
        sa = star[1][k] - 35.0
        heat = (-0.5 * THERMAL_COEF * CABBELING_T) * ta - MIXED_COEF * sa - THERMAL_COEF * (1.0 + THERMOBARIC_T * z)
        salt = (-0.5 * HALINE_COEF * CABBELING_S) * sa + HALINE_COEF * (1.0 - THERMOBARIC_S * z)
        dens.append(heat * ta + salt * sa)
    above = None
    ratio = []
    values = ([], [])
    for k in range(NK):
        if k < NK - 1:
            below = jnp.where(wet[k + 1], 5.5 - 5.0 * jnp.tanh(dens[k + 1] - dens[k]), 0.0)
            pivot = 1.0 + below
        else:
            below = None
            pivot = 1.0
        if k > 0:
            pivot = pivot + above * (1.0 - ratio[-1])
        r = pl.reciprocal(pivot, approx=True)
        r = r * (2.0 - pivot * r)
        if below is not None:
            ratio.append(below * r)
        for n in range(2):
            x = star[n][k]
            if k > 0:
                x = x + above * values[n][-1]
            values[n].append(x * r)
        above = below
    for n in range(2):
        x = values[n][NK - 1]
        outs[n][NK - 1, to, :] = jnp.where(wet[NK - 1], x, 0.0)
        for k in range(NK - 2, -1, -1):
            x = values[n][k] + ratio[k] * x
            outs[n][k, to, :] = jnp.where(wet[k], x, 0.0)


def even_row():
    return lax.rem(lax.axis_index("ja"), 2) == 0


def first_kernel(
    t_ref, s_ref, u_ref, v_ref, w_hbm, k_ref, ts_in, ss_in, own_ref, east_ref, p2_ref, west_ref,
    tn_ref, sn_ref, ts_ref, ss_ref, zonal_ref, rows_ref, merid_ref, *scratch,
):
    done_first = bulk_first()

    @pl.when(jnp.logical_not(done_first))
    def _():
        bulk_fluxes(t_ref, s_ref, u_ref, v_ref, w_hbm, k_ref, ts_ref, ss_ref, *scratch)

    lane = lanes()
    level = (lane & 15).astype(F32)
    own = [own_ref[n] for n in range(21)]
    k_own = own[12:18]
    u_own = own[18:21]
    west_floor = [east_ref[5], east_ref[4]] + k_own[3:6]
    east_floor = k_own[0:3] + [west_ref[4], west_ref[5]]
    for n in range(2):
        q = own[6 * n : 6 * n + 6]
        f0, f1 = edge_fluxes(level, [east_ref[2 * n + 1], east_ref[2 * n]] + q[3:6], west_floor, (east_ref[6], u_own[2]))
        f2, f3 = edge_fluxes(level, q[0:3] + [west_ref[2 * n], west_ref[2 * n + 1]], east_floor, (u_own[0], u_own[1]))
        parts = (f2, f3 - f2, f1 - f0, -f1)
        for r in range(4):
            x = parts[0] if r == 0 else pltpu.roll(parts[0], (0 - r) % NI, 1)
            for i in range(1, 4):
                moved = parts[i] if i == r else pltpu.roll(parts[i], (i - r) % NI, 1)
                x = jnp.where((lane & 3) == i, moved, x)
            zonal_ref[n, r] = x

    def stars(n, k, at):
        return jnp.where(done_first, (ts_in, ss_in)[n][k, at, :], (ts_ref, ss_ref)[n][k, at, :])

    folded = lax.axis_index("ja") == lax.axis_size("ja") - 1
    south = even_row()
    edge_rows(south, folded, t_ref, s_ref, v_ref, k_ref, p2_ref, rows_ref, merid_ref)
    base = jnp.where(south, 0, LAST)
    outs = (tn_ref, sn_ref)
    solve_rows(jnp.where(south, 0, NJ - EDGE), EDGE, south, k_ref, zonal_ref, merid_ref, stars, outs, base)
    solve_rows(jnp.where(south, EDGE, LAST), NJ - EDGE - LAST, south, k_ref, zonal_ref, None, stars, outs, base)


def most_rows(t, s, u, v, w, floor, ts, ss, *edges):
    vmem = pl.BlockSpec(memory_space=pltpu.VMEM)
    hbm = pl.BlockSpec(memory_space=pltpu.HBM)
    w = pltpu.with_memory_space_constraint(w, pltpu.HBM)
    return pl.pallas_call(
        first_kernel,
        out_shape=(pltpu.VMEM((NK, NJ - LAST, NI), F32),) * 2
        + (pltpu.VMEM((NK, NJ, NI), F32),) * 2
        + (pltpu.VMEM((2, 4, 8, NI), F32),),
        in_specs=[vmem] * 4 + [hbm] + [vmem] * (3 + len(edges)),
        out_specs=(vmem,) * 5,
        scratch_shapes=[pltpu.VMEM((9, NK, NI), F32), pltpu.VMEM((2, NK, 8, NI), F32)] + bulk_scratch(),
        compiler_params=pltpu.CompilerParams(vmem_limit_bytes=24 * 2**20),
        cost_estimate=pl.CostEstimate(flops=16_000_000, bytes_accessed=4_000_000, transcendentals=150_000),
        name="solve_most_rows",
    )(t, s, u, v, w, floor, ts, ss, *edges)


def second_kernel(
    t_ref, s_ref, v_ref, k_ref, ts_in, ss_in, ts_late, ss_late, zonal_ref, tn_ref, sn_ref, p1_ref, tn_hbm, sn_hbm,
    to_ref, so_ref, rows_ref, merid_ref, sems,
):
    south = jnp.logical_not(even_row())
    other = pl.ds(pl.multiple_of(jnp.where(south, LAST, 0), 8), NJ - LAST)
    start = jnp.where(south, 0, NJ - LAST)
    mine = pl.ds(pl.multiple_of(start, 8), LAST)
    first = [pltpu.make_async_copy(tn_ref, tn_hbm.at[:, other], sems.at[0]), pltpu.make_async_copy(sn_ref, sn_hbm.at[:, other], sems.at[1])]
    for c in first:
        c.start()
    done_first = bulk_first()

    def stars(n, k, at):
        return jnp.where(done_first, (ts_in, ss_in)[n][k, at, :], (ts_late, ss_late)[n][k, at, :])

    edge_rows(south, None, t_ref, s_ref, v_ref, k_ref, p1_ref, rows_ref, merid_ref)
    solve_rows(start, LAST, south, k_ref, zonal_ref, merid_ref, stars, (to_ref, so_ref), start)
    second = [pltpu.make_async_copy(to_ref, tn_hbm.at[:, mine], sems.at[2]), pltpu.make_async_copy(so_ref, sn_hbm.at[:, mine], sems.at[3])]
    for c in second:
        c.start()
    for c in first + second:
        c.wait()


def last_rows(*operands):
    vmem = pl.BlockSpec(memory_space=pltpu.VMEM)
    hbm = pl.BlockSpec(memory_space=pltpu.HBM)
    edge = pltpu.VMEM((NK, LAST, NI), F32)
    return pl.pallas_call(
        second_kernel,
        out_shape=(jax.ShapeDtypeStruct((NK, NJ, NI), F32),) * 2,
        in_specs=[vmem] * len(operands),
        out_specs=(hbm, hbm),
        scratch_shapes=[
            edge,
            edge,
            pltpu.VMEM((9, NK, NI), F32),
            pltpu.VMEM((2, NK, 8, NI), F32),
            pltpu.SemaphoreType.DMA((4,)),
        ],
        compiler_params=pltpu.CompilerParams(vmem_limit_bytes=24 * 2**20),
        cost_estimate=pl.CostEstimate(flops=3_000_000, bytes_accessed=2_000_000, transcendentals=150_000),
        name="solve_edge_rows",
    )(*operands)


def local(nj, ni, t, s, u, v, w, floor):
    p2, east, west, p1, own, t, s, u, v, floor, ts, ss = pack(t, s, u, v, w, floor)
    first = []
    second = []
    for i in range(ni):
        for j in range(0, nj, 2):
            first += [(j * ni + i, (j + 1) * ni + i), ((j + 1) * ni + i, j * ni + i)]
        for j in range(1, nj - 1, 2):
            second += [(j * ni + i, (j + 1) * ni + i), ((j + 1) * ni + i, j * ni + i)]
        second.append(((nj - 1) * ni + i, (nj - 1) * ni + ni - 1 - i))
    p1 = lax.ppermute(p1, ("ja", "ia"), first)
    p2 = lax.ppermute(p2, ("ja", "ia"), second)
    from_west = lax.ppermute(east, "ia", [(i, (i + 1) % ni) for i in range(ni)])
    from_east = lax.ppermute(west, "ia", [((i + 1) % ni, i) for i in range(ni)])
    tn, sn, ts_late, ss_late, zonal = most_rows(t, s, u, v, w, floor, ts, ss, own, from_west, p2, from_east)
    return last_rows(t, s, v, floor, ts, ss, ts_late, ss_late, zonal, tn, sn, p1)


def solution(mesh):
    field = P(None, "ja", "ia")
    return jax.shard_map(
        functools.partial(local, mesh.shape["ja"], mesh.shape["ia"]),
        mesh=mesh,
        in_specs=(field,) * 5 + (P("ja", "ia"),),
        out_specs=(field, field),
        check_vma=False,
    )
```

```python
import functools

import jax
import jax.numpy as jnp
from jax import lax
from jax.experimental import pallas as pl
from jax.experimental.pallas import tpu as pltpu
from jax.sharding import PartitionSpec as P

THERMAL_COEF = 0.1655
HALINE_COEF = 0.76554
CABBELING_T = 0.05952
CABBELING_S = 0.00054914
THERMOBARIC_T = 0.0001497
THERMOBARIC_S = 1.109e-05
MIXED_COEF = 0.0024341
LAYER_DEPTH = 50.0

NK = 16
NJ = 64
NI = 128
NB = NJ // 8
EDGE = NJ // 2
LAST = 16
F32 = jnp.float32

COLS = (-3, -2, -1, 0, 1, 2)
MROWS = 88


def lanes():
    return lax.broadcasted_iota(jnp.int32, (8, NI), 1)


def sublanes():
    return lax.broadcasted_iota(jnp.int32, (8, NI), 0)


def minmod(x, y):
    return jnp.maximum(jnp.minimum(x, jnp.maximum(y, 0.0)), jnp.minimum(y, 0.0))


def slope_factor(c):
    return jnp.where(c > 0, 0.5, -0.5) - 0.5 * c


def flux(c, c_open, factor, qa, sa, qb, sb):
    up = c > 0
    return c_open * (jnp.where(up, qa, qb) + factor * jnp.where(up, sa, sb))


def bulk_fluxes(t_ref, s_ref, u_ref, v_ref, w_hbm, k_ref, to_ref, so_ref, w_ref, th_ref, sh_ref, mask_ref, sem):
    w_copy = pltpu.make_async_copy(w_hbm, w_ref, sem)
    w_copy.start()
    lane = lanes()
    sub = sublanes()
    floors = [k_ref[pl.ds(m, 8, stride=8), :] for m in range(NB)]
    for m in range(NB):
        east = jnp.where(lane == NI - 1, 0, jnp.minimum(floors[m], pltpu.roll(floors[m], NI - 1, 1)))
        if m < NB - 1:
            north = jnp.minimum(floors[m], floors[m + 1])
        else:
            north = jnp.where(sub == 7, 0, jnp.minimum(floors[m], pltpu.roll(floors[0], 7, 0)))
        mask_ref[0, m] = east
        mask_ref[1, m] = jnp.where((lane == 0) | (lane == NI - 2), 0, east)
        mask_ref[2, m] = north
        inner = north
        if m == 0:
            inner = jnp.where(sub == 0, 0, inner)
        if m == NB - 2:
            inner = jnp.where(sub == 7, 0, inner)
        mask_ref[3, m] = inner

    def level(k):
        q = [[ref[k, pl.ds(m, 8, stride=8), :] for m in range(NB)] for ref in (t_ref, s_ref)]
        c = [v_ref[k, pl.ds(m, 8, stride=8), :] for m in range(NB)]
        c_open = [jnp.where(mask_ref[3, m] > k, c[m], 0.0) for m in range(NB)]
        is_open = [mask_ref[2, m] > k for m in range(NB)]
        factor = [slope_factor(x) for x in c]
        left = []
        for x in q:
            after = x[1:] + [pltpu.roll(x[0], 7, 0)]
            g = [jnp.where(o, b - a, 0.0) for o, a, b in zip(is_open, x, after)]
            g_before = [pltpu.roll(g[-1], 1, 0)] + g[:-1]
            slope = [minmod(a, b) for a, b in zip(g, g_before)]
            slope_after = slope[1:] + [pltpu.roll(slope[0], 7, 0)]
            f = [flux(*y) for y in zip(c, c_open, factor, x, slope, after, slope_after)]
            f_before = [pltpu.roll(f[-1], 1, 0)] + f[:-1]
            left.append([a - (b - d) for a, b, d in zip(x, f, f_before)])
        for m in range(NB):
            c = u_ref[k, pl.ds(m, 8, stride=8), :]
            c_open = jnp.where(mask_ref[1, m] > k, c, 0.0)
            is_open = mask_ref[0, m] > k
            factor = slope_factor(c)
            for n, out in ((0, th_ref), (1, sh_ref)):
                x = q[n][m]
                after = pltpu.roll(x, NI - 1, 1)
                g = jnp.where(is_open, after - x, 0.0)
                slope = minmod(g, pltpu.roll(g, 1, 1))
                f = flux(c, c_open, factor, x, slope, after, pltpu.roll(slope, NI - 1, 1))
                out[k, pl.ds(m, 8, stride=8), :] = left[n][m] - (f - pltpu.roll(f, 1, 1))

    @pl.loop(0, NK, unroll=4)
    def _(k):
        level(k)

    w_copy.wait()

    def column(b, _):
        at = pl.ds(pl.multiple_of(b * 8, 8), 8)
        floor = k_ref[at, :]
        c = [w_ref[k, at, :] for k in range(NK - 1)]
        is_open = [floor > k + 1 for k in range(NK - 1)]
        c_open = [jnp.where(o, x, 0.0) for o, x in zip(is_open, c)]
        factor = [slope_factor(x) for x in c]
        for src, half, out in ((t_ref, th_ref, to_ref), (s_ref, sh_ref, so_ref)):
            x = [src[k, at, :] for k in range(NK)]
            g = [jnp.where(is_open[k], x[k + 1] - x[k], 0.0) for k in range(NK - 1)]
            slope = [jnp.zeros((8, NI), F32)] + [minmod(g[k], g[k - 1]) for k in range(1, NK - 1)] + [jnp.zeros((8, NI), F32)]
            before = None
            for k in range(NK):
                y = half[k, at, :]
                if k < NK - 1:
                    f = flux(c[k], c_open[k], factor[k], x[k], slope[k], x[k + 1], slope[k + 1])
                    y = y - (f if before is None else f - before)
                    before = f
                else:
                    y = y + before
                out[k, at, :] = y
        return 0

    lax.fori_loop(0, NB, column, 0)


def bulk_scratch():
    field = pltpu.VMEM((NK, NJ, NI), F32)
    return [field, field, field, pltpu.VMEM((4, NB, 8, NI), jnp.int32), pltpu.SemaphoreType.DMA(())]


def bulk_first():
    ja, ia = lax.axis_index("ja"), lax.axis_index("ia")
    ni = lax.axis_size("ia")
    near_fold = ja >= lax.axis_size("ja") - 2
    return ia < jnp.where(near_fold, 3 * ni // 8, ni // 8)


def pack_kernel(
    t_hbm, s_hbm, u_hbm, v_hbm, w_hbm, k_hbm, p2_ref, east_ref, west_ref, p1_ref, own_ref,
    t_ref, s_ref, u_ref, v_ref, k_ref, ts_ref, ss_ref, sems, *scratch,
):
    chunks = 2
    per = NK // chunks
    copies = []
    for c in range(chunks):
        part = pl.ds(c * per, per)
        for f, (src, dst) in enumerate(((t_hbm, t_ref), (s_hbm, s_ref), (u_hbm, u_ref))):
            copies.append(pltpu.make_async_copy(src.at[part], dst.at[part], sems.at[c * 3 + f]))
    early = [
        pltpu.make_async_copy(k_hbm, k_ref, sems.at[12]),
        pltpu.make_async_copy(v_hbm, v_ref, sems.at[13]),
    ]
    for c in early + copies:
        c.start()

    lane = lanes()
    even = lax.rem(lax.axis_index("ja"), 2) == 0
    near1 = jnp.where(even, NJ - 1, 0)
    far1 = jnp.where(even, NJ - 2, 1)
    near2 = jnp.where(even, 0, NJ - 1)
    far2 = jnp.where(even, 1, NJ - 2)
    rows = ((p1_ref, near1, far1), (p2_ref, near2, far2))

    def windows(blocks, k, window):
        out = pltpu.roll(blocks[0], k, 1)
        for b in range(1, NB):
            out = jnp.where(window == b, pltpu.roll(blocks[b], b * 16 + k, 1), out)
        return out

    early[0].wait()
    place = (lane + 3) & (NI - 1)
    floor = windows([k_ref[pl.ds(8 * b, 8), :].astype(F32) for b in range(NB)], 0, lax.shift_right_logical(place, 4))
    first = (lane & 15) == 0
    k_cols = []
    for n, off in enumerate(COLS):
        x = jnp.where(first, pltpu.roll(floor, -off % NI, 1), 0.0)
        for step in (1, 2, 4, 8):
            x = x + pltpu.roll(x, step, 1)
        k_cols.append(x)
    early[1].wait()
    for ref, near, far in rows:
        for k in range(NK):
            ref[pl.ds(64 + k, 1), :] = v_ref[k, pl.ds(near, 1), :]
        ref[pl.ds(80, 8), :] = jnp.zeros((8, NI), F32)
        ref[pl.ds(80, 1), :] = k_ref[pl.ds(near, 1), :].astype(F32)
        ref[pl.ds(81, 1), :] = k_ref[pl.ds(far, 1), :].astype(F32)

    t_acc = [None] * 6
    s_acc = [None] * 6
    u_acc = [None] * 6
    for k in range(NK):
        if k % per == 0:
            for c in copies[k // per * 3 : k // per * 3 + 3]:
                c.wait()
        place = (lane - (k - 3)) & (NI - 1)
        window = lax.shift_right_logical(place, 4)
        within = place & 15
        for ref, acc, which in ((t_ref, t_acc, range(6)), (s_ref, s_acc, range(6)), (u_ref, u_acc, (1, 2, 3))):
            got = windows([ref[k, pl.ds(8 * b, 8), :] for b in range(NB)], k, window)
            for n in which:
                acc[n] = got if k == 0 else jnp.where(within == n, got, acc[n])
        for ref, near, far in rows:
            ref[pl.ds(k, 1), :] = t_ref[k, pl.ds(near, 1), :]
            ref[pl.ds(16 + k, 1), :] = t_ref[k, pl.ds(far, 1), :]
            ref[pl.ds(32 + k, 1), :] = s_ref[k, pl.ds(near, 1), :]
            ref[pl.ds(48 + k, 1), :] = s_ref[k, pl.ds(far, 1), :]
    t_cols = [pltpu.roll(x, -off % NI, 1) for x, off in zip(t_acc, COLS)]
    s_cols = [pltpu.roll(x, -off % NI, 1) for x, off in zip(s_acc, COLS)]
    u_cols = [pltpu.roll(u_acc[n], -COLS[n] % NI, 1) for n in (1, 2, 3)]
    for n, x in enumerate(t_cols + s_cols + k_cols + u_cols):
        own_ref[n] = x
    for n, x in enumerate((t_cols[2], t_cols[1], s_cols[2], s_cols[1], k_cols[2], k_cols[1], u_cols[1])):
        east_ref[n] = x
    for n, x in enumerate((t_cols[3], t_cols[4], s_cols[3], s_cols[4], k_cols[3], k_cols[4])):
        west_ref[n] = x

    @pl.when(bulk_first())
    def _():
        bulk_fluxes(t_ref, s_ref, u_ref, v_ref, w_hbm, k_ref, ts_ref, ss_ref, *scratch)


def pack(t, s, u, v, w, floor):
    fields = [pltpu.with_memory_space_constraint(x, pltpu.HBM) for x in (t, s, u, v, w, floor)]
    return pl.pallas_call(
        pack_kernel,
        out_shape=tuple(
            pltpu.VMEM(shape, F32) for shape in ((MROWS, NI), (11, 8, NI), (11, 8, NI), (MROWS, NI), (21, 8, NI))
        )
        + (pltpu.VMEM((NK, NJ, NI), F32),) * 4
        + (pltpu.VMEM((NJ, NI), jnp.int32),)
        + (pltpu.VMEM((NK, NJ, NI), F32),) * 2,
        in_specs=[pl.BlockSpec(memory_space=pltpu.HBM)] * 6,
        out_specs=(pl.BlockSpec(memory_space=pltpu.VMEM),) * 12,
        scratch_shapes=[pltpu.SemaphoreType.DMA((14,))] + bulk_scratch(),
        compiler_params=pltpu.CompilerParams(vmem_limit_bytes=16 * 2**20),
        name="pack_edges",
    )(*fields)


def edge_fluxes(level, q, floor, c):
    is_open = [level < jnp.minimum(a, b) for a, b in zip(floor, floor[1:])]
    g = [jnp.where(o, b - a, 0.0) for o, a, b in zip(is_open, q, q[1:])]
    slope = [None] + [minmod(a, b) for a, b in zip(g, g[1:])]
    out = []
    for n, x in zip((1, 2), c):
        out.append(flux(x, jnp.where(is_open[n], x, 0.0), slope_factor(x), q[n], slope[n], q[n + 1], slope[n + 1]))
    return out


def edge_rows(south, folded, t_ref, s_ref, v_ref, k_ref, msg_ref, rows_ref, merid_ref):
    lane = lanes()
    base = jnp.where(south, 0, NJ - 3)
    for k in range(NK):
        for n, ref in enumerate((t_ref, s_ref, v_ref)):
            for r in range(3):
                rows_ref[3 * n + r, pl.ds(k, 1), :] = ref[k, pl.ds(base + r, 1), :]

    level = lax.broadcasted_iota(jnp.int32, (NK, NI), 0).astype(F32)
    msg = [msg_ref[pl.ds(8 * n, 8), :] for n in range(MROWS // 8)]
    if folded is not None:
        turned = NI - 1 - lane
        msg = [jnp.where(folded, jnp.take_along_axis(x, turned, axis=1), x) for x in msg]

    def plane(n):
        return jnp.concatenate([msg[2 * n], msg[2 * n + 1]], axis=0)

    def wide(row):
        return jnp.broadcast_to(row, (NK, NI))

    def in_order(own, near, far):
        return [jnp.where(south, x, y) for x, y in zip([far, near] + own, own + [near, far])]

    floors = in_order([wide(k_ref[pl.ds(base + r, 1), :].astype(F32)) for r in range(3)], wide(msg[10][0:1]), wide(msg[10][1:2]))
    last = rows_ref[8]
    if folded is not None:
        last = jnp.where(folded, 0.5 * (last - plane(4)), last)
    courant = (jnp.where(south, plane(4), rows_ref[7]), jnp.where(south, rows_ref[6], last))
    merid_ref[...] = jnp.zeros_like(merid_ref)
    at_row = jnp.where(south, 0, 6)
    for n in range(2):
        q = in_order([rows_ref[3 * n + r] for r in range(3)], plane(2 * n), plane(2 * n + 1))
        f0, f1 = edge_fluxes(level, q, floors, courant)
        for i, x in enumerate((jnp.where(south, f1 - f0, f0), jnp.where(south, -f1, f1 - f0))):
            for k in range(NK):
                merid_ref[n, k, pl.ds(at_row + i, 1), :] = x[k : k + 1]


def solve_rows(start, count, south, k_ref, zonal_ref, merid_ref, stars, outs, first_row):
    lane = lanes()
    edge_lanes = (lane < 2) | (lane >= NI - 2)
    at = pl.ds(pl.multiple_of(start, 8), count)
    to = pl.ds(pl.multiple_of(start - first_row, 8), count)
    floor = k_ref[at, :]
    wet = [floor > k for k in range(NK)]
    star = []
    for n in range(2):
        star.append([])
        for k in range(NK):
            corrections = []
            for h in range(count // 8):
                c = start // 8 + h
                z = pltpu.roll(zonal_ref[n, k % 4], lax.rem(2 * NI - 2 - 4 * (k // 4) - 16 * c, NI), 1)
                z = jnp.where(edge_lanes, z, 0.0)
                if merid_ref is not None and count == 8:
                    z = z + merid_ref[n, k]
                elif merid_ref is not None and h in (0, count // 8 - 1):
                    z = z + jnp.where(south if h == 0 else jnp.logical_not(south), merid_ref[n, k], 0.0)
                corrections.append(z)
            star[n].append(jnp.where(wet[k], stars(n, k, at) - jnp.concatenate(corrections, axis=0), 0.0))
    dens = []
    for k in range(NK):
        z = LAYER_DEPTH * (k + 0.5)
        ta = star[0][k] - 10.0
        sa = star[1][k] - 35.0
        heat = (-0.5 * THERMAL_COEF * CABBELING_T) * ta - MIXED_COEF * sa - THERMAL_COEF * (1.0 + THERMOBARIC_T * z)
        salt = (-0.5 * HALINE_COEF * CABBELING_S) * sa + HALINE_COEF * (1.0 - THERMOBARIC_S * z)
        dens.append(heat * ta + salt * sa)
    above = None
    ratio = []
    values = ([], [])
    for k in range(NK):
        if k < NK - 1:
            below = jnp.where(wet[k + 1], 5.5 - 5.0 * jnp.tanh(dens[k + 1] - dens[k]), 0.0)
            pivot = 1.0 + below
        else:
            below = None
            pivot = 1.0
        if k > 0:
            pivot = pivot + above * (1.0 - ratio[-1])
        r = pl.reciprocal(pivot, approx=True)
        r = r * (2.0 - pivot * r)
        if below is not None:
            ratio.append(below * r)
        for n in range(2):
            x = star[n][k]
            if k > 0:
                x = x + above * values[n][-1]
            values[n].append(x * r)
        above = below
    for n in range(2):
        x = values[n][NK - 1]
        outs[n][NK - 1, to, :] = jnp.where(wet[NK - 1], x, 0.0)
        for k in range(NK - 2, -1, -1):
            x = values[n][k] + ratio[k] * x
            outs[n][k, to, :] = jnp.where(wet[k], x, 0.0)


def even_row():
    return lax.rem(lax.axis_index("ja"), 2) == 0


def first_kernel(
    t_ref, s_ref, u_ref, v_ref, w_hbm, k_ref, ts_in, ss_in, own_ref, east_ref, p2_ref, west_ref,
    tn_ref, sn_ref, ts_ref, ss_ref, zonal_ref, rows_ref, merid_ref, *scratch,
):
    done_first = bulk_first()

    @pl.when(jnp.logical_not(done_first))
    def _():
        bulk_fluxes(t_ref, s_ref, u_ref, v_ref, w_hbm, k_ref, ts_ref, ss_ref, *scratch)

    lane = lanes()
    level = (lane & 15).astype(F32)
    own = [own_ref[n] for n in range(21)]
    k_own = own[12:18]
    u_own = own[18:21]
    west_floor = [east_ref[5], east_ref[4]] + k_own[3:6]
    east_floor = k_own[0:3] + [west_ref[4], west_ref[5]]
    for n in range(2):
        q = own[6 * n : 6 * n + 6]
        f0, f1 = edge_fluxes(level, [east_ref[2 * n + 1], east_ref[2 * n]] + q[3:6], west_floor, (east_ref[6], u_own[2]))
        f2, f3 = edge_fluxes(level, q[0:3] + [west_ref[2 * n], west_ref[2 * n + 1]], east_floor, (u_own[0], u_own[1]))
        parts = (f2, f3 - f2, f1 - f0, -f1)
        for r in range(4):
            x = parts[0] if r == 0 else pltpu.roll(parts[0], (0 - r) % NI, 1)
            for i in range(1, 4):
                moved = parts[i] if i == r else pltpu.roll(parts[i], (i - r) % NI, 1)
                x = jnp.where((lane & 3) == i, moved, x)
            zonal_ref[n, r] = x

    def stars(n, k, at):
        return jnp.where(done_first, (ts_in, ss_in)[n][k, at, :], (ts_ref, ss_ref)[n][k, at, :])

    folded = lax.axis_index("ja") == lax.axis_size("ja") - 1
    south = even_row()
    edge_rows(south, folded, t_ref, s_ref, v_ref, k_ref, p2_ref, rows_ref, merid_ref)
    base = jnp.where(south, 0, LAST)
    outs = (tn_ref, sn_ref)
    solve_rows(jnp.where(south, 0, NJ - EDGE), EDGE, south, k_ref, zonal_ref, merid_ref, stars, outs, base)
    solve_rows(jnp.where(south, EDGE, LAST), NJ - EDGE - LAST, south, k_ref, zonal_ref, None, stars, outs, base)


def most_rows(t, s, u, v, w, floor, ts, ss, *edges):
    vmem = pl.BlockSpec(memory_space=pltpu.VMEM)
    hbm = pl.BlockSpec(memory_space=pltpu.HBM)
    w = pltpu.with_memory_space_constraint(w, pltpu.HBM)
    return pl.pallas_call(
        first_kernel,
        out_shape=(pltpu.VMEM((NK, NJ - LAST, NI), F32),) * 2
        + (pltpu.VMEM((NK, NJ, NI), F32),) * 2
        + (pltpu.VMEM((2, 4, 8, NI), F32),),
        in_specs=[vmem] * 4 + [hbm] + [vmem] * (3 + len(edges)),
        out_specs=(vmem,) * 5,
        scratch_shapes=[pltpu.VMEM((9, NK, NI), F32), pltpu.VMEM((2, NK, 8, NI), F32)] + bulk_scratch(),
        compiler_params=pltpu.CompilerParams(vmem_limit_bytes=24 * 2**20),
        cost_estimate=pl.CostEstimate(flops=16_000_000, bytes_accessed=4_000_000, transcendentals=150_000),
        name="solve_most_rows",
    )(t, s, u, v, w, floor, ts, ss, *edges)


def second_kernel(
    t_ref, s_ref, v_ref, k_ref, ts_in, ss_in, ts_late, ss_late, zonal_ref, tn_ref, sn_ref, p1_ref, tn_hbm, sn_hbm,
    to_ref, so_ref, rows_ref, merid_ref, sems,
):
    south = jnp.logical_not(even_row())
    other = pl.ds(pl.multiple_of(jnp.where(south, LAST, 0), 8), NJ - LAST)
    start = jnp.where(south, 0, NJ - LAST)
    mine = pl.ds(pl.multiple_of(start, 8), LAST)
    first = [pltpu.make_async_copy(tn_ref, tn_hbm.at[:, other], sems.at[0]), pltpu.make_async_copy(sn_ref, sn_hbm.at[:, other], sems.at[1])]
    for c in first:
        c.start()
    done_first = bulk_first()

    def stars(n, k, at):
        return jnp.where(done_first, (ts_in, ss_in)[n][k, at, :], (ts_late, ss_late)[n][k, at, :])

    edge_rows(south, None, t_ref, s_ref, v_ref, k_ref, p1_ref, rows_ref, merid_ref)
    solve_rows(start, LAST, south, k_ref, zonal_ref, merid_ref, stars, (to_ref, so_ref), start)
    second = [pltpu.make_async_copy(to_ref, tn_hbm.at[:, mine], sems.at[2]), pltpu.make_async_copy(so_ref, sn_hbm.at[:, mine], sems.at[3])]
    for c in second:
        c.start()
    for c in first + second:
        c.wait()


def last_rows(*operands):
    vmem = pl.BlockSpec(memory_space=pltpu.VMEM)
    hbm = pl.BlockSpec(memory_space=pltpu.HBM)
    edge = pltpu.VMEM((NK, LAST, NI), F32)
    return pl.pallas_call(
        second_kernel,
        out_shape=(jax.ShapeDtypeStruct((NK, NJ, NI), F32),) * 2,
        in_specs=[vmem] * len(operands),
        out_specs=(hbm, hbm),
        scratch_shapes=[
            edge,
            edge,
            pltpu.VMEM((9, NK, NI), F32),
            pltpu.VMEM((2, NK, 8, NI), F32),
            pltpu.SemaphoreType.DMA((4,)),
        ],
        compiler_params=pltpu.CompilerParams(vmem_limit_bytes=24 * 2**20),
        cost_estimate=pl.CostEstimate(flops=3_000_000, bytes_accessed=2_000_000, transcendentals=150_000),
        name="solve_edge_rows",
    )(*operands)


def local(nj, ni, t, s, u, v, w, floor):
    p2, east, west, p1, own, t, s, u, v, floor, ts, ss = pack(t, s, u, v, w, floor)
    first = []
    second = []
    for i in range(ni):
        for j in range(0, nj, 2):
            first += [(j * ni + i, (j + 1) * ni + i), ((j + 1) * ni + i, j * ni + i)]
        for j in range(1, nj - 1, 2):
            second += [(j * ni + i, (j + 1) * ni + i), ((j + 1) * ni + i, j * ni + i)]
        second.append(((nj - 1) * ni + i, (nj - 1) * ni + ni - 1 - i))
    p1 = lax.ppermute(p1, ("ja", "ia"), first)
    p2 = lax.ppermute(p2, ("ja", "ia"), second)
    from_west = lax.ppermute(east, "ia", [(i, (i + 1) % ni) for i in range(ni)])
    from_east = lax.ppermute(west, "ia", [((i + 1) % ni, i) for i in range(ni)])
    tn, sn, ts_late, ss_late, zonal = most_rows(t, s, u, v, w, floor, ts, ss, own, from_west, p2, from_east)
    return last_rows(t, s, v, floor, ts, ss, ts_late, ss_late, zonal, tn, sn, p1)


def solution(mesh):
    field = P(None, "ja", "ia")
    return jax.shard_map(
        functools.partial(local, mesh.shape["ja"], mesh.shape["ia"]),
        mesh=mesh,
        in_specs=(field,) * 5 + (P("ja", "ia"),),
        out_specs=(field, field),
        check_vma=False,
    )
```
